32 devices in a mesh: groups: 2 (over y), tensor: 8 (over z, x), section: 2 (over core).
Axes of the slice: x: 2, y: 2, z: 4, core: 2. Of those that a mesh axis runs over, the one named last changes fastest.
Arguments:
- hidden_in: bfloat16 [256, 8192], P('groups', 'tensor'), parts along dimension 0, may hold values from -6 to 6
- cotangent: bfloat16 [256, 8192], P('groups', 'tensor'), parts along dimension 0, may hold values from -0.119628906 to 0.119628906
- norm_gain: float32 [2, 8192], P('section', 'tensor'), may hold values from 0.5 to 1.5
- value_weight: bfloat16 [2, 8192, 1024], P('section', 'tensor'), may hold values from -0.0625 to 0.0625
- output_weight: bfloat16 [2, 8192, 8192], P('section', 'tensor'), may hold values from -0.0625 to 0.0625
- rotation: float32 [2, 128, 128], P('section'), may hold values from -0.5 to 1
- attention: bfloat16 [2, 4, 64, 4096], P('section', 'groups'), parts along dimension 1, may hold values from 0 to 1, as said below
Outputs:
- rotation_grad: float32 [2, 256, 128], P('section', 'groups'), parts along dimension 1
- rotation_new: float32 [2, 256, 128], P('section', 'groups'), parts along dimension 1
The draws below stay inside these ranges and needn't reach their ends.
There are 2 independent parts, one for each index of `groups`. The reference program is written for one: setup_inputs(seed, part) draws one part's arguments, and reference() takes and returns one part's arrays. A program takes and returns all parts, laid end to end along the dimension named above; an argument that names none is the same for every part. Nothing has to cross between parts.
Inputs may be any that keep to these rules, and one draw needn't show every extreme that they name: `attention`: each aligned block of 64 entries is one query's row over keys and is causal: nonnegative at and below the diagonal, zero above it, and sums to one.
All inputs are finite; a program needn't handle non-finite values.
Results may differ from the reference program's by a relative error of at most 0.013.
Values may be sent and summed in bfloat16 or wider, within the bound.
No kernel may reach another device: no remote copies, remote signals or barrier semaphores. Data moves between devices by JAX's collectives and lax.ppermute only.
A program may use at most 320 MiB of HBM per device.

```python
import jax
import jax.numpy as jnp
from jax import lax

D = 8192
HEADS = 64
KV_HEADS = 8
HEAD_DIM = 128
SEQ = 64
MBS = 2
LAYERS = 2
TOKENS = 128


def draw_rotation(key, part):
    noise_draw = jnp.clip(jax.random.normal(key, (LAYERS, HEAD_DIM, HEAD_DIM), jnp.float32), -4.0, 4.0)
    return jnp.eye(HEAD_DIM, dtype=jnp.float32)[None] + 0.06 * (noise_draw - jnp.swapaxes(noise_draw, 1, 2))


def draw_attention(key, part):
    dims_all = (LAYERS, MBS, HEADS, SEQ, SEQ)
    logits = 2.0 * jax.random.normal(key, dims_all, jnp.float32)
    causal = jnp.arange(SEQ)[:, None] >= jnp.arange(SEQ)[None, :]
    masked = jnp.where(causal, logits, -1e+30)
    row_peak = jnp.max(masked, axis=-1, keepdims=True)
    raised = jnp.where(causal, jnp.exp(masked - row_peak), 0.0)
    probs = raised / jnp.sum(raised, axis=-1, keepdims=True)
    return probs.reshape(LAYERS, MBS, HEADS, SEQ * SEQ).astype(jnp.bfloat16)


def level_of(rng, extent, shards, least, top_value):
    factor_of = 1.0
    for axis_at, shards_of in shards:
        draws = jax.random.uniform(jax.random.fold_in(jax.random.fold_in(rng, 6), axis_at), (shards_of,), jnp.float32, least / len(shards), top_value / len(shards))
        factor_of = factor_of * jnp.repeat(jnp.exp(draws), extent[axis_at] // shards_of).reshape((-1,) + (1,) * (len(extent) - 1 - axis_at))
    return factor_of


def gaussian(key, dims, scale, reach, pieces=(), kind=jnp.bfloat16):
    factor_of = level_of(key, dims, pieces, -0.22, 0.18) if pieces else 1.0
    array = jax.random.normal(key, dims, jnp.float32) * scale * factor_of
    return jnp.minimum(jnp.maximum(array, -reach), reach).astype(kind)


def setup_inputs(seed: int = 0, part: int = 0) -> dict:
    seeds = jax.random.split(jax.random.key(seed), 8)
    part_keys = jax.random.split(jax.random.fold_in(seeds[7], part), 8)
    return {
        "hidden_in": gaussian(part_keys[0], (TOKENS, D), 1.0, 6.0, ((1, 8),)),
        "cotangent": gaussian(part_keys[1], (TOKENS, D), 0.02, 0.119628906, ((1, 8),)),
        "norm_gain": jnp.clip(1.0 + 0.1 * jax.random.normal(seeds[2], (LAYERS, D), jnp.float32), 0.5, 1.5),
        "value_weight": gaussian(seeds[3], (LAYERS, D, KV_HEADS * HEAD_DIM), D ** -0.5, 0.0625, ((0, 2), (1, 8))),
        "output_weight": gaussian(seeds[4], (LAYERS, D, HEADS * HEAD_DIM), (HEADS * HEAD_DIM) ** -0.5, 0.0625, ((0, 2), (1, 8))),
        "rotation": draw_rotation(jax.random.fold_in(seeds[7], 71), part),
        "attention": draw_attention(jax.random.fold_in(jax.random.fold_in(seeds[7], part), 71), part),
    }


quant_levels = 7.0
full_turn = 6.283185307179586
norm_eps = 1e-05
scale_eps = 1e-06
step_size = 0.1
precise = lax.Precision.HIGHEST

def soft_quant(rotated):
    col_scale = (lax.optimization_barrier(jnp.max(jnp.abs(rotated), axis=0)) + scale_eps) / quant_levels
    ratio_vals = rotated / col_scale
    return (col_scale * (ratio_vals - jnp.sin(full_turn * ratio_vals) / full_turn), ratio_vals)

def cayley(rot_grad, rotation_mat):
    skew_part = jnp.dot(rot_grad, rotation_mat.T, precision=precise) - jnp.dot(rotation_mat, rot_grad.T, precision=precise)
    update = rotation_mat - step_size * jnp.dot(skew_part, rotation_mat, precision=precise)
    for sweep_idx in range(2):
        update = rotation_mat - 0.5 * step_size * jnp.dot(skew_part, rotation_mat + update, precision=precise)
    return update

def mix_heads(attn_probs, values, kv_count):
    block_count = attn_probs.shape[0]
    head_count = attn_probs.shape[1]
    seq_len = attn_probs.shape[2]
    head_dim = values.shape[1] // kv_count
    grouped = attn_probs.astype(jnp.float32).reshape(block_count, kv_count, head_count // kv_count, seq_len, seq_len)
    value_blocks = values.astype(jnp.float32).reshape(block_count, seq_len, kv_count, head_dim)
    mixed_heads = jnp.einsum('bgkqs,bsgd->bqgkd', grouped, value_blocks)
    return mixed_heads.reshape(block_count * seq_len, head_count * head_dim).astype(jnp.bfloat16)

def reference(hidden_in, cotangent, norm_gain, value_weight, output_weight, rotation, attention):
    kv_width = KV_HEADS * HEAD_DIM
    mixed_width = HEADS * HEAD_DIM
    per_group = HEADS // KV_HEADS
    stream = hidden_in
    saved_layers = []
    for layer_idx in range(LAYERS):
        rotation_mat = rotation[layer_idx]
        value_wide = value_weight[layer_idx].astype(jnp.float32).reshape(D, KV_HEADS, HEAD_DIM)
        value_rot = jnp.einsum('dgk,kj->dgj', value_wide, rotation_mat, precision=precise).reshape(D, kv_width)
        value_q, value_ratio = soft_quant(value_rot)
        value_eff = value_q.astype(jnp.bfloat16)
        out_wide = output_weight[layer_idx].astype(jnp.float32).reshape(D, HEADS, HEAD_DIM)
        out_rot = jnp.einsum('chk,kj->hjc', out_wide, rotation_mat, precision=precise).reshape(mixed_width, D)
        out_q, out_ratio = soft_quant(out_rot)
        out_eff = out_q.astype(jnp.bfloat16)
        gain_row = norm_gain[layer_idx]
        widened = stream.astype(jnp.float32)
        inverse_rms = lax.rsqrt(lax.optimization_barrier(jnp.sum(widened * widened, axis=1, keepdims=True)) / D + norm_eps)
        normed = (widened * inverse_rms * gain_row).astype(jnp.bfloat16)
        values = jnp.dot(normed, value_eff, preferred_element_type=jnp.float32).astype(jnp.bfloat16)
        layer_probs = attention[layer_idx].reshape(MBS, HEADS, SEQ, SEQ)
        mixed_heads = mix_heads(layer_probs, values, KV_HEADS)
        stream = (widened + jnp.dot(mixed_heads, out_eff, preferred_element_type=jnp.float32)).astype(jnp.bfloat16)
        saved_layers.append((value_wide, value_eff, value_ratio, out_wide, out_eff, out_ratio, widened, inverse_rms, normed, mixed_heads))
    incoming = cotangent
    grads = [None] * LAYERS
    news = [None] * LAYERS
    for layer_idx in range(LAYERS - 1, -1, -1):
        value_wide, value_eff, value_ratio, out_wide, out_eff, out_ratio, widened, inverse_rms, normed, mixed_heads = saved_layers[layer_idx]
        gain_row = norm_gain[layer_idx]
        attn_probs = attention[layer_idx].reshape(MBS, HEADS, SEQ, SEQ).astype(jnp.float32)
        out_grad = jnp.dot(mixed_heads.T, incoming, preferred_element_type=jnp.float32)
        mix_grad = jnp.dot(incoming, out_eff.T, preferred_element_type=jnp.float32).astype(jnp.bfloat16)
        grad_blocks = mix_grad.astype(jnp.float32).reshape(MBS, SEQ, HEADS, HEAD_DIM)
        head_term = jnp.einsum('bhqs,bqhd->bshd', attn_probs, grad_blocks).astype(jnp.bfloat16)
        value_grad = head_term.astype(jnp.float32).reshape(TOKENS, KV_HEADS, per_group, HEAD_DIM).sum(axis=2)
        value_grad = value_grad.reshape(TOKENS, kv_width).astype(jnp.bfloat16)
        value_grad_w = jnp.dot(normed.T, value_grad, preferred_element_type=jnp.float32)
        normed_grad = jnp.dot(value_grad, value_eff.T, preferred_element_type=jnp.float32)
        incoming = (incoming.astype(jnp.float32) + inverse_rms * gain_row * normed_grad).astype(jnp.bfloat16)
        out_slope = out_grad * (1.0 - jnp.cos(full_turn * out_ratio))
        value_slope = value_grad_w * (1.0 - jnp.cos(full_turn * value_ratio))
        rot_grad = jnp.einsum('chk,hjc->kj', out_wide, out_slope.reshape(HEADS, HEAD_DIM, D), precision=precise)
        rot_grad = rot_grad + jnp.einsum('dgk,dgj->kj', value_wide, value_slope.reshape(D, KV_HEADS, HEAD_DIM), precision=precise)
        grads[layer_idx] = rot_grad
        news[layer_idx] = cayley(rot_grad, rotation[layer_idx])
    return (jnp.stack(grads), jnp.stack(news))
```

```python
import functools

import jax
import jax.numpy as jnp
from jax import lax
from jax.experimental import pallas as pl
from jax.experimental.pallas import tpu as pltpu
from jax.sharding import PartitionSpec as P

quant_levels = 7.0
norm_eps = 1e-05
scale_eps = 1e-06
step_size = 0.1
precise = lax.Precision.HIGHEST
F32 = jnp.float32
BF16 = jnp.bfloat16
LANES = 128
VMEM_BYTES = 56 * 1024 * 1024

sin_coefs = (3.141582078119497, -5.16714420271071, 2.541908924984016, -0.5546570710297597)
cos_coefs = (0.31830775207531137, -1.570521249499652, 1.2863806003857212, -0.38901512525748255)


def dot_nn(a, b):
    return lax.dot_general(a, b, (((1,), (0,)), ((), ())), preferred_element_type=F32)


def dot_nt(a, b):
    return lax.dot_general(a, b, (((1,), (1,)), ((), ())), preferred_element_type=F32)


def dot_tn(a, b):
    return lax.dot_general(a, b, (((0,), (0,)), ((), ())), preferred_element_type=F32)


def horner(coefs, z):
    total = coefs[-1] * z + coefs[-2]
    for coef in coefs[-3::-1]:
        total = total * z + coef
    return total


def soft_parts(ratio):
    whole = jnp.round(ratio)
    rest = ratio - whole
    square = rest * rest
    sine = rest * horner(sin_coefs, square)
    cosine = horner(cos_coefs, square)
    return whole + (rest - sine * cosine), sine * sine


def rotation_pair(rot):
    high = rot.astype(BF16)
    low = (rot - high.astype(F32)).astype(BF16)
    zero = jnp.zeros_like(high)

    def blocks(part):
        return jnp.concatenate(
            [jnp.concatenate([part, zero], 1), jnp.concatenate([zero, part], 1)], 0
        )

    return blocks(high), blocks(low)


def column_of(row):
    count = row.shape[1]
    return jnp.transpose(jnp.broadcast_to(row, (count, count)))


def call(kernel, out_shape, cost, **kw):
    flops, moved = cost
    return pl.pallas_call(
        kernel,
        out_shape=out_shape,
        compiler_params=pltpu.CompilerParams(vmem_limit_bytes=VMEM_BYTES),
        cost_estimate=pl.CostEstimate(flops=flops, bytes_accessed=moved, transcendentals=0),
        **kw,
    )


def shaped(shape, dtype):
    return jax.ShapeDtypeStruct(shape, dtype)


def value_rot_kernel(hidden_ref, ct_ref, value_ref, rot_ref, x_ref, ct_t_ref, vrot_ref, stat_ref):
    kv_width = value_ref.shape[1]
    high, low = rotation_pair(rot_ref[...])
    for at in range(0, kv_width, 2 * LANES):
        cols = slice(at, at + 2 * LANES)
        block = value_ref[:, cols]
        turned = dot_nn(block, high) + dot_nn(block, low)
        vrot_ref[:, cols] = turned
        stat_ref[:, cols] = jnp.max(jnp.abs(turned), axis=0, keepdims=True)
    x = jnp.transpose(hidden_ref[...].astype(F32))
    x_ref[...] = x.astype(BF16)
    stat_ref[:, kv_width:] = jnp.sum(x * x, axis=0, keepdims=True)
    ct_t_ref[...] = jnp.transpose(ct_ref[...].astype(F32)).astype(BF16)


def mix_back(probs_ref, grad_of, out_ref, seq, per_group, kv_count):
    blocks = probs_ref.shape[0]
    for b in range(blocks):
        rows = slice(b * seq, (b + 1) * seq)
        for k in range(kv_count):
            stacked = jnp.concatenate(
                [
                    grad_of(rows, slice(h * LANES, (h + 1) * LANES))
                    for h in range(k * per_group, (k + 1) * per_group)
                ],
                0,
            )
            probs = probs_ref[b, k * per_group * seq : (k + 1) * per_group * seq, :]
            out_ref[rows, k * LANES : (k + 1) * LANES] = dot_tn(probs, stacked).astype(
                out_ref.dtype
            )


def mix_forward(probs_ref, values_of, mixed_ref, seq, per_group, kv_count):
    blocks = probs_ref.shape[0]
    for b in range(blocks):
        rows = slice(b * seq, (b + 1) * seq)
        for k in range(kv_count):
            probs = probs_ref[b, k * per_group * seq : (k + 1) * per_group * seq, :]
            heads = dot_nn(probs, values_of(rows, slice(k * LANES, (k + 1) * LANES))).astype(BF16)
            for j in range(per_group):
                h = k * per_group + j
                mixed_ref[rows, h * LANES : (h + 1) * LANES] = heads[j * seq : (j + 1) * seq]


def prep_kernel(
    kv_count, w_ref, rot_ref, ct_ref, probs_ref,
    q_ref, slope_ref, scale_ref, back_ref, vg_ref,
    turned_ref, inv_ref, total_ref,
):
    rows, width = w_ref.shape
    high, low = rotation_pair(rot_ref[...])
    peak = jnp.zeros((rows, 2 * LANES), F32)
    for at in range(0, width, 2 * LANES):
        cols = slice(at, at + 2 * LANES)
        block = w_ref[:, cols]
        turned = dot_nn(block, high) + dot_nn(block, low)
        turned_ref[:, cols] = turned
        peak = jnp.maximum(peak, jnp.abs(turned))
    peak = jnp.max(peak, axis=1, keepdims=True)
    scale = (peak + scale_eps) / quant_levels
    scale_ref[...] = scale
    inv_ref[...] = jnp.broadcast_to(1.0 / scale, inv_ref.shape)
    step, span = 16, min(512, width)

    @pl.loop(0, rows // step)
    def _(i):
        here = pl.ds(pl.multiple_of(i * step, step), step)
        inv = inv_ref[here, :1]
        for at in range(0, width, span):
            cols = slice(at, at + span)
            effective, slope = soft_parts(turned_ref[here, cols] * inv)
            q_ref[here, cols] = effective.astype(BF16)
            slope_ref[here, cols] = slope.astype(BF16)

    scaled = (ct_ref[...].astype(F32) * scale).astype(BF16)

    @pl.when(pl.program_id(0) == 0)
    def _():
        total_ref[...] = jnp.zeros_like(total_ref)

    wide = min(1024, width)
    for at in range(0, width, wide):
        cols = slice(at, at + wide)
        total_ref[:, cols] += dot_tn(scaled, q_ref[:, cols])

    @pl.when(pl.program_id(0) == pl.num_programs(0) - 1)
    def _():
        back_ref[...] = total_ref[...].astype(BF16)
        seq = probs_ref.shape[2]
        per_group = width // LANES // kv_count
        mix_back(
            probs_ref, lambda r, c: back_ref[r, c], vg_ref, seq, per_group, kv_count
        )


def value_quant_kernel(
    turned_ref, stats_ref, x_ref, gain_ref, q_ref, slope_ref, part_ref, scale_ref, mean_ref, *, model_width
):
    kv_width = turned_ref.shape[1]
    stats = stats_ref[...]
    scale = (jnp.max(stats[:, :kv_width], axis=0, keepdims=True) + scale_eps) / quant_levels
    scale_ref[...] = scale
    squares = jnp.sum(stats[:, kv_width:], axis=0, keepdims=True)
    mean_ref[...] = lax.rsqrt(squares / model_width + norm_eps)
    inv = 1.0 / scale
    step = 16

    @pl.loop(0, turned_ref.shape[0] // step)
    def _(i):
        here = pl.ds(pl.multiple_of(i * step, step), step)
        effective, slope = soft_parts(turned_ref[here, :] * inv)
        q_ref[here, :] = effective.astype(BF16)
        slope_ref[here, :] = slope.astype(BF16)

    gained = (x_ref[...].astype(F32) * gain_ref[...]).astype(BF16)
    part_ref[...] = dot_tn(gained, q_ref[...]).astype(BF16)


def input_grad_kernel(vg_ref, scale_ref, q_ref, gain_ref, out_ref):
    scaled = (vg_ref[...].astype(F32) * scale_ref[...]).astype(BF16)
    out_ref[...] = (dot_nt(q_ref[...], scaled) * gain_ref[...]).astype(BF16)


def forward_kernel(
    kv_count, values_ref, mean_ref, vscale_ref, probs_ref, q_ref, scale_ref, x_ref, grad_ref,
    mixed_ref, out_ref, back_ref, total_ref, v_ref,
):
    first = pl.program_id(0) == 0
    width = q_ref.shape[1]
    seq = probs_ref.shape[2]
    per_group = width // LANES // kv_count

    @pl.when(first)
    def _():
        total_ref[...] = jnp.zeros_like(total_ref)
        inverse = column_of(mean_ref[...])
        for k in range(kv_count):
            cols = slice(k * LANES, (k + 1) * LANES)
            v_ref[:, cols] = (
                values_ref[:, cols].astype(F32) * inverse[:, :1] * vscale_ref[:, cols]
            ).astype(BF16)
        mix_forward(probs_ref, lambda r, c: v_ref[r, c], mixed_ref, seq, per_group, kv_count)

    scale = scale_ref[...]
    out_ref[...] = (x_ref[...].astype(F32) + dot_nt(q_ref[...], mixed_ref[...]) * scale).astype(BF16)
    scaled = (grad_ref[...].astype(F32) * scale).astype(BF16)
    wide = min(1024, width)
    for at in range(0, width, wide):
        cols = slice(at, at + wide)
        total_ref[:, cols] += dot_tn(scaled, q_ref[:, cols])

    @pl.when(pl.program_id(0) == pl.num_programs(0) - 1)
    def _():
        back_ref[...] = total_ref[...].astype(BF16)


def project_kernel(x_ref, gain_ref, q_ref, out_ref):
    kv_width = q_ref.shape[1]
    x = x_ref[...].astype(F32)
    gained = (x * gain_ref[...]).astype(BF16)
    out_ref[:, :kv_width] = dot_tn(gained, q_ref[...]).astype(BF16)
    squares = jnp.sum(x * x, axis=0, keepdims=True)
    tokens = squares.shape[1]
    out_ref[:, kv_width:] = jnp.broadcast_to(squares, (tokens, tokens)).astype(BF16)


def value_grad_kernel(kv_count, mean_ref, ct_back_ref, back_ref, probs_ref, out_ref):
    inverse = column_of(mean_ref[...])[:, :1]
    seq = probs_ref.shape[2]
    per_group = back_ref.shape[1] // LANES // kv_count

    def grad_of(rows, cols):
        return (
            ct_back_ref[rows, cols].astype(F32) + inverse[rows] * back_ref[rows, cols].astype(F32)
        ).astype(BF16)

    mix_back(probs_ref, grad_of, out_ref, seq, per_group, kv_count)


def out_grad_kernel(
    kv_count, section_ref, values_ref, mean_ref, vscale_ref, probs_ref, mixed_in_ref,
    ct_ref, grad_ref, w_ref, slope_ref, out_ref, mixed_ref, total_ref,
):
    width = w_ref.shape[1]
    seq = probs_ref.shape[2]
    per_group = width // LANES // kv_count
    last_section = section_ref[0] != 0

    @pl.when(pl.program_id(0) == 0)
    def _():
        total_ref[...] = jnp.zeros_like(total_ref)

        @pl.when(last_section)
        def _():
            inverse = column_of(mean_ref[...])[:, :1]

            def values_of(rows, cols):
                return (
                    values_ref[rows, cols].astype(F32) * inverse[rows] * vscale_ref[:, cols]
                ).astype(BF16)

            mix_forward(probs_ref, values_of, mixed_ref, seq, per_group, kv_count)

        @pl.when(jnp.logical_not(last_section))
        def _():
            mixed_ref[...] = mixed_in_ref[...]

    keep = jnp.where(last_section, 0.0, 1.0)
    grad = (
        ct_ref[...].astype(F32) + (keep * mean_ref[...]) * grad_ref[...].astype(F32)
    ).astype(BF16)
    for at in range(0, width, 2 * LANES):
        cols = slice(at, at + 2 * LANES)
        out_grad = dot_nn(grad, mixed_ref[:, cols])
        sloped = (out_grad * slope_ref[:, cols].astype(F32)).astype(BF16)
        total_ref[...] += dot_tn(w_ref[:, cols], sloped)

    @pl.when(pl.program_id(0) == pl.num_programs(0) - 1)
    def _():
        out_ref[...] = total_ref[:LANES, :LANES] + total_ref[LANES:, LANES:]


def value_part_kernel(x_ref, mean_ref, gain_ref, vg_ref, v_ref, slope_ref, other_ref, out_ref):
    normed = (x_ref[...].astype(F32) * mean_ref[...] * gain_ref[...]).astype(BF16)
    total = other_ref[...]
    for at in range(0, v_ref.shape[1], 2 * LANES):
        cols = slice(at, at + 2 * LANES)
        grad = dot_nn(normed, vg_ref[:, cols])
        sloped = (grad * slope_ref[:, cols].astype(F32)).astype(BF16)
        both = dot_tn(v_ref[:, cols], sloped)
        total = total + both[:LANES, :LANES] + both[LANES:, LANES:]
    out_ref[...] = (2.0 * total).astype(out_ref.dtype)


def cayley_kernel(parts_ref, rot_ref, grad_ref, new_ref):
    count = parts_ref.shape[0] // LANES
    grad = parts_ref[:LANES].astype(F32)
    for i in range(1, count):
        grad = grad + parts_ref[i * LANES : (i + 1) * LANES].astype(F32)
    grad_ref[...] = grad
    rot = rot_ref[...]

    def product(a, b, dims=(1, 0)):
        return lax.dot_general(
            a, b, (((dims[0],), (dims[1],)), ((), ())), precision=precise, preferred_element_type=F32
        )

    turn = product(grad, rot, (1, 1))
    skew = turn - jnp.transpose(turn)
    update = rot - step_size * product(skew, rot)
    for _ in range(2):
        update = rot - 0.5 * step_size * product(skew, rot + update)
    new_ref[...] = update


def exchange(rows):
    return lax.all_to_all(rows, "tensor", split_axis=0, concat_axis=0, tiled=True)


def on_device(hidden, cotangent, norm_gain, value_weight, output_weight, rotation, attention):
    section = lax.axis_index("section")
    count = lax.axis_size("tensor")
    is_first = section == 0
    flag = section.astype(jnp.int32).reshape(1)
    rot = rotation[0]
    value_w = value_weight[0]
    out_w = output_weight[0]
    local, width = out_w.shape
    kv_width = value_w.shape[1]
    kv_count = kv_width // LANES
    tokens = hidden.shape[0]
    _, blocks, heads, flat = attention.shape
    seq = tokens // blocks
    probs = attention[0].reshape(blocks, heads * seq, seq)
    gain = norm_gain[0].reshape(local, 1)
    model_width = local * count
    big = 2 * tokens * local * width

    x0, ct, value_rot, stat = call(
        value_rot_kernel,
        (
            shaped((local, tokens), BF16),
            shaped((local, tokens), BF16),
            shaped((local, kv_width), F32),
            shaped((1, kv_width + tokens), F32),
        ),
        (4 * local * kv_width * LANES, 6 * local * kv_width),
    )(hidden, cotangent, value_w, rot)
    stats = lax.all_gather(stat, "tensor", axis=0, tiled=True)

    rows = min(local, 256)
    steps = local // rows

    def split(*tail):
        return pl.BlockSpec((rows,) + tail, lambda i: (i, 0))

    def whole(*shape):
        return pl.BlockSpec(shape, lambda i: (0,) * len(shape))

    quant, slope, scale, ct_back, ct_vg = call(
        functools.partial(prep_kernel, kv_count),
        (
            shaped((local, width), BF16),
            shaped((local, width), BF16),
            shaped((local, 1), F32),
            shaped((tokens, width), BF16),
            shaped((tokens, kv_width), BF16),
        ),
        (3 * big, 6 * local * width),
        grid=(steps,),
        in_specs=[split(width), whole(LANES, LANES), split(tokens), whole(*probs.shape)],
        out_specs=(
            split(width),
            split(width),
            split(1),
            whole(tokens, width),
            whole(tokens, kv_width),
        ),
        scratch_shapes=[
            pltpu.VMEM((rows, width), F32),
            pltpu.VMEM((rows, LANES), F32),
            pltpu.VMEM((tokens, width), F32),
        ],
    )(out_w, rot, ct, probs)

    value_q, value_slope, value_part, value_scale, mean0 = call(
        functools.partial(value_quant_kernel, model_width=model_width),
        (
            shaped((local, kv_width), BF16),
            shaped((local, kv_width), BF16),
            shaped((tokens, kv_width), BF16),
            shaped((1, kv_width), F32),
            shaped((1, tokens), F32),
        ),
        (2 * local * kv_width * tokens, 8 * local * kv_width),
    )(value_rot, stats, x0, gain)

    def add_parts(received):
        return received.reshape(count, tokens // count, -1).astype(F32).sum(0)

    def spread(part):
        return jnp.tile(part.astype(BF16), (count, 1))

    summed = exchange(spread(add_parts(exchange(jnp.where(is_first, value_part, ct_vg)))))

    grad1 = call(
        input_grad_kernel,
        shaped((local, tokens), BF16),
        (2 * local * kv_width * tokens, 2 * local * kv_width),
    )(summed, value_scale, value_q, gain)
    grad1 = lax.ppermute(grad1, "section", [(1, 0)])

    mixed, x1, grad_back = call(
        functools.partial(forward_kernel, kv_count),
        (
            shaped((tokens, width), BF16),
            shaped((local, tokens), BF16),
            shaped((tokens, width), BF16),
        ),
        (2 * big, 2 * local * width),
        grid=(steps,),
        in_specs=[
            whole(tokens, kv_width),
            whole(1, tokens),
            whole(1, kv_width),
            whole(*probs.shape),
            split(width),
            split(1),
            split(tokens),
            split(tokens),
        ],
        out_specs=(whole(tokens, width), split(tokens), whole(tokens, width)),
        scratch_shapes=[pltpu.VMEM((tokens, width), F32), pltpu.VMEM((tokens, kv_width), BF16)],
    )(summed, mean0, value_scale, probs, quant, scale, x0, grad1)
    arrived = lax.ppermute(x1, "section", [(0, 1)])
    x1 = jnp.where(is_first, x1, arrived)

    projected = call(
        project_kernel,
        shaped((tokens, kv_width + tokens), BF16),
        (2 * local * kv_width * tokens, 2 * local * kv_width),
    )(x1, gain, value_q)
    received = add_parts(exchange(projected))
    mean1 = lax.rsqrt(received[:1, kv_width:] / model_width + norm_eps)

    vg0 = call(
        functools.partial(value_grad_kernel, kv_count),
        shaped((tokens, kv_width), BF16),
        (2 * tokens * width * seq, 6 * tokens * width),
    )(mean1, ct_back, grad_back, probs)
    values1 = exchange(jnp.where(is_first, vg0, spread(received[:, :kv_width])))
    vg_full = exchange(spread(add_parts(values1)))

    out_part = call(
        functools.partial(out_grad_kernel, kv_count),
        shaped((LANES, LANES), F32),
        (2 * big, 4 * local * width),
        grid=(steps,),
        in_specs=[
            pl.BlockSpec(memory_space=pltpu.SMEM),
            whole(tokens, kv_width),
            whole(1, tokens),
            whole(1, kv_width),
            whole(*probs.shape),
            whole(tokens, width),
            split(tokens),
            split(tokens),
            split(width),
            split(width),
        ],
        out_specs=whole(LANES, LANES),
        scratch_shapes=[
            pltpu.VMEM((tokens, width), BF16),
            pltpu.VMEM((2 * LANES, 2 * LANES), F32),
        ],
    )(flag, values1, mean1, value_scale, probs, mixed, ct, grad1, out_w, slope)

    rot_part = call(
        value_part_kernel,
        shaped((LANES, LANES), BF16),
        (4 * local * kv_width * tokens, 4 * local * kv_width),
    )(
        jnp.where(is_first, x0, x1),
        jnp.where(is_first, mean0, mean1),
        gain,
        jnp.where(is_first, vg_full, summed),
        value_w,
        value_slope,
        out_part,
    )
    rot_grad, rot_new = call(
        cayley_kernel,
        (shaped((LANES, LANES), F32), shaped((LANES, LANES), F32)),
        (12 * 5 * LANES**3, 8 * LANES**2),
    )(exchange(jnp.tile(rot_part, (count, 1))), rot)
    return rot_grad[None], rot_new[None]


def solution(mesh):
    in_specs = (
        P("groups", "tensor"),
        P("groups", "tensor"),
        P("section", "tensor"),
        P("section", "tensor", None),
        P("section", "tensor", None),
        P("section", None, None),
        P("section", "groups", None, None),
    )
    out_specs = (P("section", "groups", None), P("section", "groups", None))
    return jax.shard_map(
        on_device, mesh=mesh, in_specs=in_specs, out_specs=out_specs, check_vma=False
    )
```

```python
import functools

import jax
import jax.numpy as jnp
from jax import lax
from jax.experimental import pallas as pl
from jax.experimental.pallas import tpu as pltpu
from jax.sharding import PartitionSpec as P

quant_levels = 7.0
norm_eps = 1e-05
scale_eps = 1e-06
step_size = 0.1
precise = lax.Precision.HIGHEST
F32 = jnp.float32
BF16 = jnp.bfloat16
LANES = 128
VMEM_BYTES = 56 * 1024 * 1024

sin_coefs = (3.141582078119497, -5.16714420271071, 2.541908924984016, -0.5546570710297597)
sin_top = sin_coefs[3]
slope_factor = 2.0 * sin_top * sin_top
unit = 1.000002 / (sin_top * sin_top)


def dot_nn(a, b):
    return lax.dot_general(a, b, (((1,), (0,)), ((), ())), preferred_element_type=F32)


def dot_nt(a, b):
    return lax.dot_general(a, b, (((1,), (1,)), ((), ())), preferred_element_type=F32)


def dot_tn(a, b):
    return lax.dot_general(a, b, (((0,), (0,)), ((), ())), preferred_element_type=F32)


def sine_scale(scale):
    return scale * (-sin_top * sin_top / 3.141592653589793)


def soft_parts(turned, inverse, factor):
    ratio = turned * inverse
    rest = ratio - jnp.round(ratio)
    square = rest * rest
    sine = rest * (
        ((square + sin_coefs[2] / sin_top) * square + sin_coefs[1] / sin_top) * square
        + sin_coefs[0] / sin_top
    )
    slope = sine * sine
    below = unit - slope
    return turned - (sine * (below * lax.rsqrt(below))) * factor, slope


def rotation_pair(rot):
    high = rot.astype(BF16)
    low = (rot - high.astype(F32)).astype(BF16)
    zero = jnp.zeros_like(high)

    def blocks(part):
        return jnp.concatenate(
            [jnp.concatenate([part, zero], 1), jnp.concatenate([zero, part], 1)], 0
        )

    return blocks(high), blocks(low)


def column_of(row):
    count = row.shape[1]
    return jnp.transpose(jnp.broadcast_to(row, (count, count)))


def call(kernel, out_shape, cost, **kw):
    flops, moved = cost
    return pl.pallas_call(
        kernel,
        out_shape=out_shape,
        compiler_params=pltpu.CompilerParams(vmem_limit_bytes=VMEM_BYTES),
        cost_estimate=pl.CostEstimate(flops=flops, bytes_accessed=moved, transcendentals=0),
        **kw,
    )


def shaped(shape, dtype):
    return jax.ShapeDtypeStruct(shape, dtype)


def value_rot_kernel(
    hidden_ref, ct_ref, gain_row_ref, value_ref, rot_ref, x_ref, ct_t_ref, gain_ref, vrot_ref, stat_ref
):
    kv_width = value_ref.shape[1]
    high, low = rotation_pair(rot_ref[...])

    @pl.when(pl.program_id(0) == 0)
    def _():
        stat_ref[...] = jnp.zeros_like(stat_ref)

    for at in range(0, kv_width, 2 * LANES):
        cols = slice(at, at + 2 * LANES)
        block = value_ref[:, cols]
        turned = dot_nn(block, high) + dot_nn(block, low)
        vrot_ref[:, cols] = turned
        peak = jnp.max(jnp.abs(turned), axis=0, keepdims=True)
        stat_ref[:, cols] = jnp.maximum(stat_ref[:, cols], peak)
    x = jnp.transpose(hidden_ref[...].astype(F32))
    x_ref[...] = x.astype(BF16)
    stat_ref[:, kv_width:] += jnp.sum(x * x, axis=0, keepdims=True)
    ct_t_ref[...] = jnp.transpose(ct_ref[...].astype(F32)).astype(BF16)
    gain_ref[...] = jnp.transpose(jnp.broadcast_to(gain_row_ref[...], hidden_ref.shape))


def mix_back(probs_ref, grad_of, out_ref, seq, per_group, kv_count):
    blocks = probs_ref.shape[0]
    for b in range(blocks):
        rows = slice(b * seq, (b + 1) * seq)
        for k in range(kv_count):
            stacked = jnp.concatenate(
                [
                    grad_of(rows, slice(h * LANES, (h + 1) * LANES))
                    for h in range(k * per_group, (k + 1) * per_group)
                ],
                0,
            )
            probs = probs_ref[b, k * per_group * seq : (k + 1) * per_group * seq, :]
            out_ref[rows, k * LANES : (k + 1) * LANES] = dot_tn(probs, stacked).astype(
                out_ref.dtype
            )


def mix_forward(probs_ref, values_of, mixed_ref, seq, per_group, kv_count):
    blocks = probs_ref.shape[0]
    for b in range(blocks):
        rows = slice(b * seq, (b + 1) * seq)
        for k in range(kv_count):
            probs = probs_ref[b, k * per_group * seq : (k + 1) * per_group * seq, :]
            heads = dot_nn(probs, values_of(rows, slice(k * LANES, (k + 1) * LANES))).astype(BF16)
            for j in range(per_group):
                h = k * per_group + j
                mixed_ref[rows, h * LANES : (h + 1) * LANES] = heads[j * seq : (j + 1) * seq]


def prep_kernel(kv_count, starts, ends, number, *refs):
    refs = list(refs)
    w_ref, rot_ref, ct_ref = refs[:3]
    del refs[:3]
    if ends:
        probs_ref = refs.pop(0)
    if not starts:
        held_ref = refs[1]
        del refs[:4]
    q_ref, slope_ref = refs[:2]
    del refs[:2]
    if ends:
        back_ref, vg_ref = refs[:2]
        del refs[:2]
    total_ref, turned_ref, inv_ref, factor_ref = refs
    rows, width = w_ref.shape
    step, last = pl.program_id(0), number - 1
    lines = 16
    wide = min(1024, width)

    @pl.when(step == 0)
    def _():
        total_ref[...] = jnp.zeros_like(total_ref) if starts else held_ref[...]

    high, low = rotation_pair(rot_ref[...])
    peak = jnp.zeros((rows, LANES), F32)
    for at in range(0, width, 2 * LANES):
        cols = slice(at, at + 2 * LANES)
        block = w_ref[:, cols]
        turned = dot_nn(block, high) + dot_nn(block, low)
        turned_ref[:, cols] = turned
        size = jnp.abs(turned)
        peak = jnp.maximum(peak, jnp.maximum(size[:, :LANES], size[:, LANES:]))
    scale = (jnp.max(peak, axis=1, keepdims=True) + scale_eps) / quant_levels
    inv_ref[...] = jnp.broadcast_to(1.0 / scale, inv_ref.shape)
    factor_ref[...] = jnp.broadcast_to(sine_scale(scale), inv_ref.shape)

    @pl.loop(0, rows // lines, unroll=2)
    def _(i):
        here = pl.ds(pl.multiple_of(i * lines, lines), lines)
        inverse, factor = inv_ref[here, :], factor_ref[here, :]
        for at in range(0, width, LANES):
            cols = slice(at, at + LANES)
            effective, slope = soft_parts(turned_ref[here, cols], inverse, factor)
            q_ref[here, cols] = effective.astype(BF16)
            slope_ref[here, cols] = slope.astype(BF16)

    for at in range(0, width, wide):
        cols = slice(at, at + wide)
        total_ref[:, cols] += dot_tn(ct_ref[...], q_ref[:, cols])

    if ends:

        @pl.when(step == last)
        def _():
            back_ref[...] = total_ref[...].astype(BF16)
            seq = probs_ref.shape[2]
            per_group = width // LANES // kv_count
            mix_back(probs_ref, lambda r, c: back_ref[r, c], vg_ref, seq, per_group, kv_count)


def value_quant_kernel(
    model_width, turned_ref, stats_ref, x_ref, gain_ref, q_ref, slope_ref, part_ref, mean_ref, total_ref
):
    kv_width = turned_ref.shape[1]
    stats = stats_ref[...]
    scale = (jnp.max(stats[:, :kv_width], axis=0, keepdims=True) + scale_eps) / quant_levels
    squares = jnp.sum(stats[:, kv_width:], axis=0, keepdims=True)
    mean = lax.rsqrt(squares / model_width + norm_eps)
    inverse = 1.0 / scale
    factor = sine_scale(scale)
    lines = 16
    inverses = [
        jnp.broadcast_to(inverse[:, at : at + LANES], (lines, LANES))
        for at in range(0, kv_width, LANES)
    ]

    @pl.loop(0, turned_ref.shape[0] // lines)
    def _(i):
        here = pl.ds(pl.multiple_of(i * lines, lines), lines)
        for j, wide in enumerate(inverses):
            cols = slice(j * LANES, (j + 1) * LANES)
            effective, slope = soft_parts(turned_ref[here, cols], wide, factor[:, cols])
            q_ref[here, cols] = effective.astype(BF16)
            slope_ref[here, cols] = slope.astype(BF16)

    @pl.when(pl.program_id(0) == 0)
    def _():
        mean_ref[...] = mean
        total_ref[...] = jnp.zeros_like(total_ref)

    normed = (x_ref[...].astype(F32) * mean * gain_ref[...]).astype(BF16)
    total_ref[...] += dot_tn(normed, q_ref[...])

    @pl.when(pl.program_id(0) == pl.num_programs(0) - 1)
    def _():
        part_ref[...] = total_ref[...].astype(BF16)


def input_grad_kernel(vg_ref, q_ref, gain_ref, out_ref):
    out_ref[...] = (dot_nt(q_ref[...], vg_ref[...]) * gain_ref[...]).astype(BF16)


def forward_kernel(kv_count, values_ref, probs_ref, q_ref, x_ref, mixed_ref, out_ref):
    @pl.when(pl.program_id(0) == 0)
    def _():
        seq = probs_ref.shape[2]
        per_group = q_ref.shape[1] // LANES // kv_count
        mix_forward(probs_ref, lambda r, c: values_ref[r, c], mixed_ref, seq, per_group, kv_count)

    out_ref[...] = (x_ref[...].astype(F32) + dot_nt(q_ref[...], mixed_ref[...])).astype(BF16)


def back_kernel(q_ref, grad_ref, back_ref, total_ref):
    width = q_ref.shape[1]

    @pl.when(pl.program_id(0) == 0)
    def _():
        total_ref[...] = jnp.zeros_like(total_ref)

    wide = min(1024, width)
    for at in range(0, width, wide):
        cols = slice(at, at + wide)
        total_ref[:, cols] += dot_tn(grad_ref[...], q_ref[:, cols])

    @pl.when(pl.program_id(0) == pl.num_programs(0) - 1)
    def _():
        back_ref[...] = total_ref[...].astype(BF16)


def project_kernel(x_ref, gain_ref, q_ref, out_ref):
    kv_width = q_ref.shape[1]
    x = x_ref[...].astype(F32)
    gained = (x * gain_ref[...]).astype(BF16)
    out_ref[:, :kv_width] = dot_tn(gained, q_ref[...]).astype(BF16)
    squares = jnp.sum(x * x, axis=0, keepdims=True)
    tokens = squares.shape[1]
    out_ref[:, kv_width:] = jnp.broadcast_to(squares, (tokens, tokens)).astype(BF16)


def value_grad_kernel(kv_count, mean_ref, ct_back_ref, back_ref, probs_ref, out_ref):
    inverse = column_of(mean_ref[...])[:, :1]
    seq = probs_ref.shape[2]
    per_group = back_ref.shape[1] // LANES // kv_count

    def grad_of(rows, cols):
        return (
            ct_back_ref[rows, cols].astype(F32) + inverse[rows] * back_ref[rows, cols].astype(F32)
        ).astype(BF16)

    mix_back(probs_ref, grad_of, out_ref, seq, per_group, kv_count)


def out_grad_kernel(
    kv_count, section_ref, values_ref, mean_ref, probs_ref, mixed_in_ref,
    ct_ref, grad_ref, w_ref, slope_ref, out_ref, mixed_ref, total_ref,
):
    width = w_ref.shape[1]
    seq = probs_ref.shape[2]
    per_group = width // LANES // kv_count
    last_section = section_ref[0] != 0

    @pl.when(pl.program_id(0) == 0)
    def _():
        total_ref[...] = jnp.zeros_like(total_ref)

        @pl.when(last_section)
        def _():
            mix_forward(
                probs_ref, lambda r, c: values_ref[r, c], mixed_ref, seq, per_group, kv_count
            )

        @pl.when(jnp.logical_not(last_section))
        def _():
            mixed_ref[...] = mixed_in_ref[...]

    keep = jnp.where(last_section, 0.0, 1.0)
    grad = (
        ct_ref[...].astype(F32) + (keep * mean_ref[...]) * grad_ref[...].astype(F32)
    ).astype(BF16)
    for at in range(0, width, 2 * LANES):
        cols = slice(at, at + 2 * LANES)
        out_grad = dot_nn(grad, mixed_ref[:, cols])
        sloped = (out_grad * slope_ref[:, cols].astype(F32)).astype(BF16)
        total_ref[...] += dot_tn(w_ref[:, cols], sloped)

    @pl.when(pl.program_id(0) == pl.num_programs(0) - 1)
    def _():
        out_ref[...] = total_ref[:LANES, :LANES] + total_ref[LANES:, LANES:]


def value_part_kernel(x_ref, mean_ref, gain_ref, vg_ref, v_ref, slope_ref, other_ref, out_ref):
    normed = (x_ref[...].astype(F32) * mean_ref[...] * gain_ref[...]).astype(BF16)
    total = other_ref[...]
    for at in range(0, v_ref.shape[1], 2 * LANES):
        cols = slice(at, at + 2 * LANES)
        grad = dot_nn(normed, vg_ref[:, cols])
        sloped = (grad * slope_ref[:, cols].astype(F32)).astype(BF16)
        both = dot_tn(v_ref[:, cols], sloped)
        total = total + both[:LANES, :LANES] + both[LANES:, LANES:]
    out_ref[...] = (slope_factor * total).astype(out_ref.dtype)


def cayley_kernel(parts_ref, rot_ref, grad_ref, new_ref):
    count = parts_ref.shape[0] // LANES
    grad = parts_ref[:LANES].astype(F32)
    for i in range(1, count):
        grad = grad + parts_ref[i * LANES : (i + 1) * LANES].astype(F32)
    grad_ref[...] = grad
    rot = rot_ref[...]

    def product(a, b, dims=(1, 0)):
        return lax.dot_general(
            a, b, (((dims[0],), (dims[1],)), ((), ())), precision=precise, preferred_element_type=F32
        )

    turn = product(grad, rot, (1, 1))
    skew = turn - jnp.transpose(turn)
    update = rot - step_size * product(skew, rot)
    for _ in range(2):
        update = rot - 0.5 * step_size * product(skew, rot + update)
    new_ref[...] = update


def exchange(rows):
    return lax.all_to_all(rows, "tensor", split_axis=0, concat_axis=0, tiled=True)


def on_device(hidden, cotangent, norm_gain, value_weight, output_weight, rotation, attention):
    section = lax.axis_index("section")
    count = lax.axis_size("tensor")
    is_first = section == 0
    flag = section.astype(jnp.int32).reshape(1)
    rot = rotation[0]
    value_w = value_weight[0]
    out_w = output_weight[0]
    local, width = out_w.shape
    kv_width = value_w.shape[1]
    kv_count = kv_width // LANES
    tokens = hidden.shape[0]
    _, blocks, heads, flat = attention.shape
    seq = tokens // blocks
    probs = attention[0].reshape(blocks, heads * seq, seq)
    model_width = local * count
    big = 2 * tokens * local * width

    def split(rows, *tail):
        return pl.BlockSpec((rows,) + tail, lambda i: (i, 0))

    def across(lines, rows):
        return pl.BlockSpec((lines, rows), lambda i: (0, i))

    def whole(*shape):
        return pl.BlockSpec(shape, lambda i: (0,) * len(shape))

    rows = min(local, 256)
    x0, ct, gain, value_rot, stat = call(
        value_rot_kernel,
        (
            shaped((local, tokens), BF16),
            shaped((local, tokens), BF16),
            shaped((local, tokens), F32),
            shaped((local, kv_width), F32),
            shaped((1, kv_width + tokens), F32),
        ),
        (4 * local * kv_width * LANES, 6 * local * kv_width),
        grid=(local // rows,),
        in_specs=[
            across(tokens, rows),
            across(tokens, rows),
            across(1, rows),
            split(rows, kv_width),
            whole(LANES, LANES),
        ],
        out_specs=(
            split(rows, tokens),
            split(rows, tokens),
            split(rows, tokens),
            split(rows, kv_width),
            whole(1, kv_width + tokens),
        ),
    )(hidden, cotangent, norm_gain, value_w, rot)
    stats = exchange(jnp.tile(stat, (count, 1)))

    part_rows = min(local, 128)
    part_count = local // part_rows

    def prepare(first, number, before):
        starts, ends = first == 0, first + number == part_count

        def ahead(lines, *tail):
            return pl.BlockSpec((lines,) + tail, lambda i: (first + i, 0))

        def behind(lines, *tail):
            return pl.BlockSpec((lines,) + tail, lambda i: (first + i, 0))

        anywhere = pl.BlockSpec(memory_space=pl.ANY)
        operands = [out_w, rot, ct]
        in_specs = [ahead(part_rows, width), whole(LANES, LANES), behind(part_rows, tokens)]
        if ends:
            operands.append(probs)
            in_specs.append(whole(*probs.shape))
        aliases = {}
        if not starts:
            quant, slope, held, after = before
            at = len(operands)
            operands += [after, held, quant, slope]
            in_specs += [anywhere, whole(tokens, width), anywhere, anywhere]
            aliases = {at + 2: 0, at + 3: 1}
        outs = [shaped((local, width), BF16), shaped((local, width), BF16)]
        out_specs = [behind(part_rows, width), behind(part_rows, width)]
        scratch = []
        if ends:
            outs += [shaped((tokens, width), BF16), shaped((tokens, kv_width), BF16)]
            out_specs += [whole(tokens, width), whole(tokens, kv_width)]
            scratch.append(pltpu.VMEM((tokens, width), F32))
        else:
            outs.append(shaped((tokens, width), F32))
            out_specs.append(whole(tokens, width))
        scratch += [
            pltpu.VMEM((part_rows, width), F32),
            pltpu.VMEM((part_rows, LANES), F32),
            pltpu.VMEM((part_rows, LANES), F32),
        ]
        return call(
            functools.partial(prep_kernel, kv_count, starts, ends, number),
            tuple(outs),
            (40 * big * number // part_count, 6 * local * width * number // part_count),
            grid=(number,),
            in_specs=in_specs,
            out_specs=tuple(out_specs),
            scratch_shapes=scratch,
            input_output_aliases=aliases,
        )(*operands)

    lead = part_count // 4
    before = prepare(0, lead, None) if lead else None

    value_q, value_slope, value_part, mean0 = call(
        functools.partial(value_quant_kernel, model_width),
        (
            shaped((local, kv_width), BF16),
            shaped((local, kv_width), BF16),
            shaped((tokens, kv_width), BF16),
            shaped((1, tokens), F32),
        ),
        (2 * local * kv_width * tokens, 8 * local * kv_width),
        grid=(local // rows,),
        in_specs=[
            split(rows, kv_width),
            whole(count, kv_width + tokens),
            split(rows, tokens),
            split(rows, tokens),
        ],
        out_specs=(
            split(rows, kv_width),
            split(rows, kv_width),
            whole(tokens, kv_width),
            whole(1, tokens),
        ),
        scratch_shapes=[pltpu.VMEM((tokens, kv_width), F32)],
    )(value_rot, stats, x0, gain)

    def add_parts(received):
        return received.reshape(count, tokens // count, -1).astype(F32).sum(0)

    def spread(part):
        return jnp.tile(part.astype(BF16), (count, 1))

    values0 = spread(add_parts(exchange(value_part)))
    if lead:
        before = tuple(before) + (value_part,)
    quant, slope, ct_back, ct_vg = prepare(lead, part_count - lead, before)

    second = exchange(jnp.where(is_first, values0, ct_vg))
    vg1 = exchange(spread(add_parts(second)))

    mixed, x1 = call(
        functools.partial(forward_kernel, kv_count),
        (shaped((tokens, width), BF16), shaped((local, tokens), BF16)),
        (big, 2 * local * width),
        grid=(local // rows,),
        in_specs=[
            whole(tokens, kv_width),
            whole(*probs.shape),
            split(rows, width),
            split(rows, tokens),
        ],
        out_specs=(whole(tokens, width), split(rows, tokens)),
    )(second, probs, quant, x0)
    arrived = lax.ppermute(x1, "section", [(0, 1)])
    x1 = jnp.where(is_first, x1, arrived)

    projected = call(
        project_kernel,
        shaped((tokens, kv_width + tokens), BF16),
        (2 * local * kv_width * tokens, 2 * local * kv_width),
    )(x1, gain, value_q)
    received = add_parts(exchange(projected))
    mean1 = lax.rsqrt(received[:1, kv_width:] / model_width + norm_eps)

    grad1 = call(
        input_grad_kernel,
        shaped((local, tokens), BF16),
        (2 * local * kv_width * tokens, 2 * local * kv_width),
    )(vg1, value_q, gain)
    grad1 = lax.ppermute(grad1, "section", [(1, 0)])
    grad_back = call(
        back_kernel,
        shaped((tokens, width), BF16),
        (big, 2 * local * width),
        grid=(local // rows,),
        in_specs=[split(rows, width), split(rows, tokens)],
        out_specs=whole(tokens, width),
        scratch_shapes=[pltpu.VMEM((tokens, width), F32)],
    )(quant, grad1)

    vg0 = call(
        functools.partial(value_grad_kernel, kv_count),
        shaped((tokens, kv_width), BF16),
        (2 * tokens * width * seq, 6 * tokens * width),
    )(mean1, ct_back, grad_back, probs)
    mine = lax.axis_index("tensor") * (tokens // count)
    own_mean = lax.dynamic_slice(mean1[0], (mine,), (tokens // count,))[:, None]
    values1 = exchange(jnp.where(is_first, vg0, spread(received[:, :kv_width] * own_mean)))
    vg0 = exchange(spread(add_parts(values1)))

    out_part = call(
        functools.partial(out_grad_kernel, kv_count),
        shaped((LANES, LANES), F32),
        (2 * big, 4 * local * width),
        grid=(local // rows,),
        in_specs=[
            pl.BlockSpec(memory_space=pltpu.SMEM),
            whole(tokens, kv_width),
            whole(1, tokens),
            whole(*probs.shape),
            whole(tokens, width),
            split(rows, tokens),
            split(rows, tokens),
            split(rows, width),
            split(rows, width),
        ],
        out_specs=whole(LANES, LANES),
        scratch_shapes=[
            pltpu.VMEM((tokens, width), BF16),
            pltpu.VMEM((2 * LANES, 2 * LANES), F32),
        ],
    )(flag, values1, mean1, probs, mixed, ct, grad1, out_w, slope)

    rot_part = call(
        value_part_kernel,
        shaped((LANES, LANES), BF16),
        (4 * local * kv_width * tokens, 4 * local * kv_width),
    )(
        jnp.where(is_first, x0, x1),
        jnp.where(is_first, mean0, mean1),
        gain,
        jnp.where(is_first, vg0, vg1),
        value_w,
        value_slope,
        out_part,
    )
    rot_grad, rot_new = call(
        cayley_kernel,
        (shaped((LANES, LANES), F32), shaped((LANES, LANES), F32)),
        (12 * 5 * LANES**3, 8 * LANES**2),
    )(exchange(jnp.tile(rot_part, (count, 1))), rot)
    return rot_grad[None], rot_new[None]


def solution(mesh):
    in_specs = (
        P("groups", "tensor"),
        P("groups", "tensor"),
        P("section", "tensor"),
        P("section", "tensor", None),
        P("section", "tensor", None),
        P("section", None, None),
        P("section", "groups", None, None),
    )
    out_specs = (P("section", "groups", None), P("section", "groups", None))
    return jax.shard_map(
        on_device, mesh=mesh, in_specs=in_specs, out_specs=out_specs, check_vma=False
    )
```

```python
import functools

import jax
import jax.numpy as jnp
from jax import lax
from jax.experimental import pallas as pl
from jax.experimental.pallas import tpu as pltpu
from jax.sharding import PartitionSpec as P

quant_levels = 7.0
norm_eps = 1e-05
scale_eps = 1e-06
step_size = 0.1
precise = lax.Precision.HIGHEST
F32 = jnp.float32
BF16 = jnp.bfloat16
LANES = 128
VMEM_BYTES = 56 * 1024 * 1024

sin_coefs = (3.141582078119497, -5.16714420271071, 2.541908924984016, -0.5546570710297597)
sin_top = sin_coefs[3]
slope_factor = 2.0 * sin_top * sin_top
unit = 1.000002 / (sin_top * sin_top)


def dot_nn(a, b):
    return lax.dot_general(a, b, (((1,), (0,)), ((), ())), preferred_element_type=F32)


def dot_nt(a, b):
    return lax.dot_general(a, b, (((1,), (1,)), ((), ())), preferred_element_type=F32)


def dot_tn(a, b):
    return lax.dot_general(a, b, (((0,), (0,)), ((), ())), preferred_element_type=F32)


def sine_scale(scale):
    return scale * (-sin_top * sin_top / 3.141592653589793)


def soft_parts(turned, inverse, factor):
    ratio = turned * inverse
    rest = ratio - jnp.round(ratio)
    square = rest * rest
    sine = rest * (
        ((square + sin_coefs[2] / sin_top) * square + sin_coefs[1] / sin_top) * square
        + sin_coefs[0] / sin_top
    )
    slope = sine * sine
    below = unit - slope
    return turned - (sine * (below * lax.rsqrt(below))) * factor, slope


def rotation_pair(rot):
    high = rot.astype(BF16)
    low = (rot - high.astype(F32)).astype(BF16)
    zero = jnp.zeros_like(high)

    def blocks(part):
        return jnp.concatenate(
            [jnp.concatenate([part, zero], 1), jnp.concatenate([zero, part], 1)], 0
        )

    return blocks(high), blocks(low)


def column_of(row):
    count = row.shape[1]
    return jnp.transpose(jnp.broadcast_to(row, (count, count)))


def call(kernel, out_shape, cost, **kw):
    flops, moved = cost
    prefetch = kw.pop("prefetch", 0)
    if prefetch:
        names = ("grid", "in_specs", "out_specs", "scratch_shapes")
        fields = {name: kw.pop(name) for name in names if name in kw}
        kw["grid_spec"] = pltpu.PrefetchScalarGridSpec(num_scalar_prefetch=prefetch, **fields)
    return pl.pallas_call(
        kernel,
        out_shape=out_shape,
        compiler_params=pltpu.CompilerParams(vmem_limit_bytes=VMEM_BYTES),
        cost_estimate=pl.CostEstimate(flops=flops, bytes_accessed=moved, transcendentals=0),
        **kw,
    )


def shaped(shape, dtype):
    return jax.ShapeDtypeStruct(shape, dtype)


def value_rot_kernel(
    hidden_ref, ct_ref, gain_row_ref, value_ref, rot_ref,
    x_ref, ct_t_ref, gain_ref, vrot_ref, stats_ref, stat_ref,
):
    kv_width = value_ref.shape[1]
    high, low = rotation_pair(rot_ref[...])

    @pl.when(pl.program_id(0) == 0)
    def _():
        stat_ref[...] = jnp.zeros_like(stat_ref)

    for at in range(0, kv_width, 2 * LANES):
        cols = slice(at, at + 2 * LANES)
        block = value_ref[:, cols]
        turned = dot_nn(block, high) + dot_nn(block, low)
        vrot_ref[:, cols] = turned
        peak = jnp.max(jnp.abs(turned), axis=0, keepdims=True)
        stat_ref[:, cols] = jnp.maximum(stat_ref[:, cols], peak)
    x = jnp.transpose(hidden_ref[...].astype(F32))
    x_ref[...] = x.astype(BF16)
    stat_ref[:, kv_width:] += jnp.sum(x * x, axis=0, keepdims=True)
    ct_t_ref[...] = jnp.transpose(ct_ref[...].astype(F32)).astype(BF16)
    gain_ref[...] = jnp.transpose(jnp.broadcast_to(gain_row_ref[...], hidden_ref.shape))

    @pl.when(pl.program_id(0) == pl.num_programs(0) - 1)
    def _():
        stats_ref[...] = jnp.broadcast_to(stat_ref[...], stats_ref.shape)


def mix_back(probs_ref, grad_of, out_ref, seq, per_group, kv_count):
    blocks = probs_ref.shape[0]
    for b in range(blocks):
        rows = slice(b * seq, (b + 1) * seq)
        for k in range(kv_count):
            stacked = jnp.concatenate(
                [
                    grad_of(rows, slice(h * LANES, (h + 1) * LANES))
                    for h in range(k * per_group, (k + 1) * per_group)
                ],
                0,
            )
            probs = probs_ref[b, k * per_group * seq : (k + 1) * per_group * seq, :]
            out_ref[rows, k * LANES : (k + 1) * LANES] = dot_tn(probs, stacked).astype(
                out_ref.dtype
            )


def mix_forward(probs_ref, values_of, mixed_ref, seq, per_group, kv_count):
    blocks = probs_ref.shape[0]
    for b in range(blocks):
        rows = slice(b * seq, (b + 1) * seq)
        for k in range(kv_count):
            probs = probs_ref[b, k * per_group * seq : (k + 1) * per_group * seq, :]
            heads = dot_nn(probs, values_of(rows, slice(k * LANES, (k + 1) * LANES))).astype(BF16)
            for j in range(per_group):
                h = k * per_group + j
                mixed_ref[rows, h * LANES : (h + 1) * LANES] = heads[j * seq : (j + 1) * seq]


def prep_kernel(kv_count, starts, ends, number, *refs):
    refs = list(refs)
    w_ref, rot_ref, ct_ref = refs[:3]
    del refs[:3]
    if ends:
        probs_ref = refs.pop(0)
    if not starts:
        held_ref = refs[1]
        del refs[:4]
    q_ref, slope_ref = refs[:2]
    del refs[:2]
    back_ref = refs.pop(0)
    if ends:
        vg_ref = refs.pop(0)
    total_ref, turned_ref, inv_ref, factor_ref = refs
    rows, width = w_ref.shape
    step, last = pl.program_id(0), number - 1
    lines = 16
    wide = min(1024, width)

    @pl.when(step == 0)
    def _():
        total_ref[...] = jnp.zeros_like(total_ref)

    high, low = rotation_pair(rot_ref[...])
    peak = jnp.zeros((rows, LANES), F32)
    for at in range(0, width, 2 * LANES):
        cols = slice(at, at + 2 * LANES)
        block = w_ref[:, cols]
        turned = dot_nn(block, high) + dot_nn(block, low)
        turned_ref[:, cols] = turned
        size = jnp.abs(turned)
        peak = jnp.maximum(peak, jnp.maximum(size[:, :LANES], size[:, LANES:]))
    scale = (jnp.max(peak, axis=1, keepdims=True) + scale_eps) / quant_levels
    inv_ref[...] = jnp.broadcast_to(1.0 / scale, inv_ref.shape)
    factor_ref[...] = jnp.broadcast_to(sine_scale(scale), inv_ref.shape)

    @pl.loop(0, rows // lines, unroll=2)
    def _(i):
        here = pl.ds(pl.multiple_of(i * lines, lines), lines)
        inverse, factor = inv_ref[here, :], factor_ref[here, :]
        for at in range(0, width, LANES):
            cols = slice(at, at + LANES)
            effective, slope = soft_parts(turned_ref[here, cols], inverse, factor)
            q_ref[here, cols] = effective.astype(BF16)
            slope_ref[here, cols] = slope.astype(BF16)

    for at in range(0, width, wide):
        cols = slice(at, at + wide)
        total_ref[:, cols] += dot_tn(ct_ref[...], q_ref[:, cols])

    if ends:

        @pl.when(step == last)
        def _():
            if not starts:
                total_ref[...] += held_ref[...].astype(F32)
            back_ref[...] = total_ref[...].astype(BF16)
            seq = probs_ref.shape[2]
            per_group = width // LANES // kv_count
            mix_back(probs_ref, lambda r, c: back_ref[r, c], vg_ref, seq, per_group, kv_count)
    else:

        @pl.when(step == last)
        def _():
            back_ref[...] = total_ref[...].astype(BF16)


def value_quant_kernel(
    model_width, turned_ref, stats_ref, x_ref, gain_ref, q_ref, slope_ref, part_ref, mean_ref, total_ref
):
    kv_width = turned_ref.shape[1]
    stats = stats_ref[...]
    scale = (jnp.max(stats[:, :kv_width], axis=0, keepdims=True) + scale_eps) / quant_levels
    squares = jnp.sum(stats[:, kv_width:], axis=0, keepdims=True)
    mean = lax.rsqrt(squares / model_width + norm_eps)
    inverse = 1.0 / scale
    factor = sine_scale(scale)
    lines = 16
    inverses = [
        jnp.broadcast_to(inverse[:, at : at + LANES], (lines, LANES))
        for at in range(0, kv_width, LANES)
    ]

    @pl.loop(0, turned_ref.shape[0] // lines)
    def _(i):
        here = pl.ds(pl.multiple_of(i * lines, lines), lines)
        for j, wide in enumerate(inverses):
            cols = slice(j * LANES, (j + 1) * LANES)
            effective, slope = soft_parts(turned_ref[here, cols], wide, factor[:, cols])
            q_ref[here, cols] = effective.astype(BF16)
            slope_ref[here, cols] = slope.astype(BF16)

    @pl.when(pl.program_id(0) == 0)
    def _():
        mean_ref[...] = mean
        total_ref[...] = jnp.zeros_like(total_ref)

    normed = (x_ref[...].astype(F32) * mean * gain_ref[...]).astype(BF16)
    total_ref[...] += dot_tn(normed, q_ref[...])

    @pl.when(pl.program_id(0) == pl.num_programs(0) - 1)
    def _():
        part_ref[...] = total_ref[...].astype(BF16)


def forward_kernel(kv_count, active_ref, values_ref, probs_ref, q_ref, x_ref, mixed_ref, out_ref):
    @pl.when(active_ref[0] == 1)
    def _():
        @pl.when(pl.program_id(0) == 0)
        def _():
            seq = probs_ref.shape[2]
            per_group = q_ref.shape[1] // LANES // kv_count
            mix_forward(
                probs_ref, lambda r, c: values_ref[r, c], mixed_ref, seq, per_group, kv_count
            )

        out_ref[...] = (x_ref[...].astype(F32) + dot_nt(q_ref[...], mixed_ref[...])).astype(BF16)


def back_kernel(active_ref, q_ref, grad_ref, after_ref, back_ref, total_ref):
    width = q_ref.shape[1]

    @pl.when(active_ref[0] == 1)
    def _():
        @pl.when(pl.program_id(0) == 0)
        def _():
            total_ref[...] = jnp.zeros_like(total_ref)

        wide = min(1024, width)
        for at in range(0, width, wide):
            cols = slice(at, at + wide)
            total_ref[:, cols] += dot_tn(grad_ref[...], q_ref[:, cols])

        @pl.when(pl.program_id(0) == pl.num_programs(0) - 1)
        def _():
            back_ref[...] = total_ref[...].astype(BF16)


def project_kernel(
    active_ref, own_ref, arrived_ref, vg_ref, gain_ref, q_ref, out_ref, grad_ref, total_ref, sum_ref
):
    kv_width = q_ref.shape[1]
    last_section = active_ref[0] == 1
    first, last = pl.program_id(0) == 0, pl.program_id(0) == pl.num_programs(0) - 1

    @pl.when(first)
    def _():
        total_ref[...] = jnp.zeros_like(total_ref)
        sum_ref[...] = jnp.zeros_like(sum_ref)

    x = jnp.where(last_section, arrived_ref[...], own_ref[...]).astype(F32)
    sum_ref[...] += jnp.sum(x * x, axis=0, keepdims=True)

    @pl.when(last_section)
    def _():
        total_ref[...] += dot_tn((x * gain_ref[...]).astype(BF16), q_ref[...])
        grad_ref[...] = (dot_nt(q_ref[...], vg_ref[...]) * gain_ref[...]).astype(BF16)

    @pl.when(last)
    def _():
        out_ref[:, :kv_width] = total_ref[...].astype(BF16)
        tokens = sum_ref.shape[1]
        out_ref[:, kv_width:] = jnp.broadcast_to(sum_ref[...], (tokens, tokens)).astype(BF16)


def value_grad_kernel(kv_count, active_ref, mean_ref, ct_back_ref, back_ref, probs_ref, out_ref, inv_ref):
    seq = probs_ref.shape[2]
    per_group = back_ref.shape[1] // LANES // kv_count

    @pl.when(active_ref[0] == 1)
    def _():
        inv_ref[...] = column_of(mean_ref[...])
        inverse = inv_ref[pl.ds(pl.multiple_of(pl.program_id(0) * seq, seq), seq), :1]

        def grad_of(rows, cols):
            return (
                ct_back_ref[rows, cols].astype(F32) + inverse * back_ref[rows, cols].astype(F32)
            ).astype(BF16)

        mix_back(probs_ref, grad_of, out_ref, seq, per_group, kv_count)


def out_grad_block(grad, mixed_ref, w_ref, slope_ref, total_ref):
    width, together = w_ref.shape[1], 8
    for first in range(0, width, 2 * LANES * together):
        pieces = []
        for at in range(first, min(first + 2 * LANES * together, width), 2 * LANES):
            cols = slice(at, at + 2 * LANES)
            out_grad = dot_nn(grad, mixed_ref[:, cols])
            sloped = (out_grad * slope_ref[:, cols].astype(F32)).astype(BF16)
            pieces.append((w_ref[:, cols], sloped))
        total_ref[...] += dot_tn(*(jnp.concatenate(side, 0) for side in zip(*pieces)))


def both_heads(total_ref):
    return total_ref[:LANES, :LANES] + total_ref[LANES:, LANES:]


def early_grad_kernel(
    section_ref, mean_ref, mixed_ref, ct_ref, grad_ref, w_ref, slope_ref, after_ref, out_ref, total_ref
):
    @pl.when(pl.program_id(0) == 0)
    def _():
        total_ref[...] = jnp.zeros_like(total_ref)

    @pl.when(section_ref[0] == 0)
    def _():
        grad = (ct_ref[...].astype(F32) + mean_ref[...] * grad_ref[...].astype(F32)).astype(BF16)
        out_grad_block(grad, mixed_ref, w_ref, slope_ref, total_ref)

    @pl.when(pl.program_id(0) == pl.num_programs(0) - 1)
    def _():
        out_ref[...] = both_heads(total_ref)


def out_grad_kernel(
    kv_count, half, section_ref, values_ref, mean_ref, probs_ref, mixed_in_ref,
    ct_ref, grad_ref, w_ref, slope_ref, other_ref, out_ref, mixed_ref, total_ref,
):
    seq = probs_ref.shape[2]
    per_group = w_ref.shape[1] // LANES // kv_count
    last_section = section_ref[0] != 0

    @pl.when(pl.program_id(0) == 0)
    def _():
        total_ref[...] = jnp.zeros_like(total_ref)

        @pl.when(last_section)
        def _():
            mix_forward(
                probs_ref, lambda r, c: values_ref[r, c], mixed_ref, seq, per_group, kv_count
            )

    @pl.when(last_section)
    def _():
        out_grad_block(ct_ref[...], mixed_ref, w_ref, slope_ref, total_ref)

    @pl.when(jnp.logical_and(section_ref[0] == 0, pl.program_id(0) >= half))
    def _():
        grad = (ct_ref[...].astype(F32) + mean_ref[...] * grad_ref[...].astype(F32)).astype(BF16)
        out_grad_block(grad, mixed_in_ref, w_ref, slope_ref, total_ref)

    @pl.when(pl.program_id(0) == pl.num_programs(0) - 1)
    def _():
        out_ref[...] = both_heads(total_ref)
        if half:
            out_ref[...] += other_ref[...]


def value_part_kernel(
    section_ref, x0_ref, x1_ref, mean0_ref, mean1_ref, gain_ref, vg0_ref, vg1_ref, v_ref, slope_ref,
    other_ref, out_ref, total_ref,
):
    first = section_ref[0] == 0
    x = jnp.where(first, x0_ref[...], x1_ref[...]).astype(F32)
    mean = jnp.where(first, mean0_ref[...], mean1_ref[...])
    normed = (x * mean * gain_ref[...]).astype(BF16)

    @pl.when(pl.program_id(0) == 0)
    def _():
        total_ref[...] = other_ref[...]

    pieces = []
    for at in range(0, v_ref.shape[1], 2 * LANES):
        cols = slice(at, at + 2 * LANES)
        grad = dot_nn(normed, jnp.where(first, vg0_ref[:, cols], vg1_ref[:, cols]))
        sloped = (grad * slope_ref[:, cols].astype(F32)).astype(BF16)
        pieces.append((v_ref[:, cols], sloped))
    both = dot_tn(*(jnp.concatenate(side, 0) for side in zip(*pieces)))
    total_ref[...] += both[:LANES, :LANES] + both[LANES:, LANES:]

    @pl.when(pl.program_id(0) == pl.num_programs(0) - 1)
    def _():
        total = (slope_factor * total_ref[...]).astype(out_ref.dtype)
        for i in range(out_ref.shape[0] // LANES):
            out_ref[i * LANES : (i + 1) * LANES] = total


def cayley_kernel(parts_ref, rot_ref, grad_ref, new_ref):
    count = parts_ref.shape[0] // LANES
    grad = parts_ref[:LANES].astype(F32)
    for i in range(1, count):
        grad = grad + parts_ref[i * LANES : (i + 1) * LANES].astype(F32)
    grad_ref[...] = grad
    rot = rot_ref[...]

    def product(a, b, dims=(1, 0)):
        return lax.dot_general(
            a, b, (((dims[0],), (dims[1],)), ((), ())), precision=precise, preferred_element_type=F32
        )

    turn = product(grad, rot, (1, 1))
    skew = turn - jnp.transpose(turn)
    update = rot - step_size * product(skew, rot)
    for _ in range(2):
        update = rot - 0.5 * step_size * product(skew, rot + update)
    new_ref[...] = update


def exchange(rows):
    return lax.all_to_all(rows, "tensor", split_axis=0, concat_axis=0, tiled=True)


def on_device(hidden, cotangent, norm_gain, value_weight, output_weight, rotation, attention):
    section = lax.axis_index("section")
    count = lax.axis_size("tensor")
    is_first = section == 0
    flag = section.astype(jnp.int32).reshape(1)
    rot = rotation[0]
    value_w = value_weight[0]
    out_w = output_weight[0]
    local, width = out_w.shape
    kv_width = value_w.shape[1]
    kv_count = kv_width // LANES
    tokens = hidden.shape[0]
    _, blocks, heads, flat = attention.shape
    seq = tokens // blocks
    probs = attention[0].reshape(blocks, heads * seq, seq)
    model_width = local * count
    big = 2 * tokens * local * width

    def split(rows, *tail):
        return pl.BlockSpec((rows,) + tail, lambda i: (i, 0))

    def across(lines, rows):
        return pl.BlockSpec((lines, rows), lambda i: (0, i))

    def whole(*shape):
        return pl.BlockSpec(shape, lambda i: (0,) * len(shape))

    rows = min(local, 256)
    x0, ct, gain, value_rot, stat = call(
        value_rot_kernel,
        (
            shaped((local, tokens), BF16),
            shaped((local, tokens), BF16),
            shaped((local, tokens), F32),
            shaped((local, kv_width), F32),
            shaped((count, kv_width + tokens), F32),
        ),
        (4 * local * kv_width * LANES, 6 * local * kv_width),
        grid=(local // rows,),
        in_specs=[
            across(tokens, rows),
            across(tokens, rows),
            across(1, rows),
            split(rows, kv_width),
            whole(LANES, LANES),
        ],
        out_specs=(
            split(rows, tokens),
            split(rows, tokens),
            split(rows, tokens),
            split(rows, kv_width),
            whole(count, kv_width + tokens),
        ),
        scratch_shapes=[pltpu.VMEM((1, kv_width + tokens), F32)],
    )(hidden, cotangent, norm_gain, value_w, rot)
    stats = exchange(stat)

    part_rows = min(local, 128)
    part_count = local // part_rows

    def prepare(first, number, before):
        starts, ends = first == 0, first + number == part_count

        def ahead(lines, *tail):
            return pl.BlockSpec((lines,) + tail, lambda i: (first + i, 0))

        def behind(lines, *tail):
            return pl.BlockSpec((lines,) + tail, lambda i: (first + i, 0))

        anywhere = pl.BlockSpec(memory_space=pl.ANY)
        operands = [out_w, rot, ct]
        in_specs = [ahead(part_rows, width), whole(LANES, LANES), behind(part_rows, tokens)]
        if ends:
            operands.append(probs)
            in_specs.append(whole(*probs.shape))
        aliases = {}
        if not starts:
            quant, slope, held, after = before
            at = len(operands)
            operands += [after, held, quant, slope]
            in_specs += [anywhere, whole(tokens, width), anywhere, anywhere]
            aliases = {at + 2: 0, at + 3: 1}
        outs = [shaped((local, width), BF16), shaped((local, width), BF16)]
        out_specs = [behind(part_rows, width), behind(part_rows, width)]
        scratch = [pltpu.VMEM((tokens, width), F32)]
        if ends:
            outs += [shaped((tokens, width), BF16), shaped((tokens, kv_width), BF16)]
            out_specs += [whole(tokens, width), whole(tokens, kv_width)]
        else:
            outs.append(shaped((tokens, width), BF16))
            out_specs.append(whole(tokens, width))
        scratch += [
            pltpu.VMEM((part_rows, width), F32),
            pltpu.VMEM((part_rows, LANES), F32),
            pltpu.VMEM((part_rows, LANES), F32),
        ]
        return call(
            functools.partial(prep_kernel, kv_count, starts, ends, number),
            tuple(outs),
            (40 * big * number // part_count, 6 * local * width * number // part_count),
            grid=(number,),
            in_specs=in_specs,
            out_specs=tuple(out_specs),
            scratch_shapes=scratch,
            input_output_aliases=aliases,
        )(*operands)

    lead = part_count // 4
    before = prepare(0, lead, None) if lead else None

    value_q, value_slope, value_part, mean0 = call(
        functools.partial(value_quant_kernel, model_width),
        (
            shaped((local, kv_width), BF16),
            shaped((local, kv_width), BF16),
            shaped((tokens, kv_width), BF16),
            shaped((1, tokens), F32),
        ),
        (2 * local * kv_width * tokens, 8 * local * kv_width),
        grid=(local // rows,),
        in_specs=[
            split(rows, kv_width),
            whole(count, kv_width + tokens),
            split(rows, tokens),
            split(rows, tokens),
        ],
        out_specs=(
            split(rows, kv_width),
            split(rows, kv_width),
            whole(tokens, kv_width),
            whole(1, tokens),
        ),
        scratch_shapes=[pltpu.VMEM((tokens, kv_width), F32)],
    )(value_rot, stats, x0, gain)

    def add_parts(received):
        return received.reshape(count, tokens // count, -1).astype(F32).sum(0)

    def spread(part):
        return jnp.tile(part.astype(BF16), (count, 1))

    values0 = spread(add_parts(exchange(value_part)))
    if lead:
        before = tuple(before) + (value_part,)
    quant, slope, ct_back, ct_vg = prepare(lead, part_count - lead, before)

    on_first = 1 - flag
    anywhere = pl.BlockSpec(memory_space=pl.ANY)

    def only(lines, *tail):
        return pl.BlockSpec((lines,) + tail, lambda i, active: (i * active[0], 0))

    def each(lines, *tail):
        return pl.BlockSpec((lines,) + tail, lambda i, active: (i, 0))

    def fixed(*shape):
        return pl.BlockSpec(shape, lambda i, active: (0,) * len(shape))

    second = exchange(jnp.where(is_first, values0, ct_vg))
    second, to_gather = lax.optimization_barrier((second, spread(add_parts(second))))
    vg1 = exchange(to_gather)

    mixed, x1 = call(
        functools.partial(forward_kernel, kv_count),
        (shaped((tokens, width), BF16), shaped((local, tokens), BF16)),
        (big, 2 * local * width),
        prefetch=1,
        grid=(local // rows,),
        in_specs=[
            fixed(tokens, kv_width),
            fixed(*probs.shape),
            only(rows, width),
            only(rows, tokens),
        ],
        out_specs=(fixed(tokens, width), only(rows, tokens)),
    )(on_first, second, probs, quant, x0)
    arrived = lax.ppermute(x1, "section", [(0, 1)])

    half_rows = max(local // 2, min(local, 128))
    projected, grad1 = call(
        project_kernel,
        (shaped((tokens, kv_width + tokens), BF16), shaped((local, tokens), BF16)),
        (4 * local * kv_width * tokens, 2 * local * kv_width),
        prefetch=1,
        grid=(local // half_rows,),
        in_specs=[
            each(half_rows, tokens),
            each(half_rows, tokens),
            fixed(tokens, kv_width),
            each(half_rows, tokens),
            only(half_rows, kv_width),
        ],
        out_specs=(fixed(tokens, kv_width + tokens), only(half_rows, tokens)),
        scratch_shapes=[pltpu.VMEM((tokens, kv_width), F32), pltpu.VMEM((1, tokens), F32)],
    )(flag, x1, arrived, vg1, gain, value_q)
    received = add_parts(exchange(projected))
    mean1 = lax.rsqrt(received[:1, kv_width:] / model_width + norm_eps)

    grad1 = lax.ppermute(grad1, "section", [(1, 0)])
    grad_back = call(
        back_kernel,
        shaped((tokens, width), BF16),
        (big, 2 * local * width),
        prefetch=1,
        grid=(local // rows,),
        in_specs=[only(rows, width), only(rows, tokens), anywhere],
        out_specs=fixed(tokens, width),
        scratch_shapes=[pltpu.VMEM((tokens, width), F32)],
    )(on_first, quant, grad1, projected)

    vg0 = call(
        functools.partial(value_grad_kernel, kv_count),
        shaped((tokens, kv_width), BF16),
        (2 * tokens * width * seq, 6 * tokens * width),
        prefetch=1,
        grid=(blocks,),
        in_specs=[
            fixed(1, tokens),
            each(seq, width),
            each(seq, width),
            pl.BlockSpec((1, heads * seq, seq), lambda i, active: (i, 0, 0)),
        ],
        out_specs=each(seq, kv_width),
        scratch_shapes=[pltpu.VMEM((tokens, tokens), F32)],
    )(on_first, mean1, ct_back, grad_back, probs)
    mine = lax.axis_index("tensor") * (tokens // count)
    own_mean = lax.dynamic_slice(mean1[0], (mine,), (tokens // count,))[:, None]
    to_send = jnp.where(is_first, vg0, spread(received[:, :kv_width] * own_mean))
    values1 = exchange(to_send)

    def early(lines, *tail):
        return pl.BlockSpec((lines,) + tail, lambda i, section: (i * (1 - section[0]), 0))

    half = part_count // 2
    pair_total = pltpu.VMEM((2 * LANES, 2 * LANES), F32)
    out_part = jnp.zeros((LANES, LANES), F32)
    if half:
        out_part = call(
            early_grad_kernel,
            shaped((LANES, LANES), F32),
            (big, 2 * local * width),
            prefetch=1,
            grid=(half,),
            in_specs=[
                fixed(1, tokens),
                fixed(tokens, width),
                early(part_rows, tokens),
                early(part_rows, tokens),
                early(part_rows, width),
                early(part_rows, width),
                anywhere,
            ],
            out_specs=fixed(LANES, LANES),
            scratch_shapes=[pair_total],
        )(flag, mean1, mixed, ct, grad1, out_w, slope, to_send)
        values1, out_part = lax.optimization_barrier((values1, out_part))
    vg0 = exchange(spread(add_parts(values1)))

    def late(lines, *tail):
        return pl.BlockSpec(
            (lines,) + tail, lambda i, section: (jnp.maximum(i, (1 - section[0]) * half), 0)
        )

    out_part = call(
        functools.partial(out_grad_kernel, kv_count, half),
        shaped((LANES, LANES), F32),
        (2 * big, 4 * local * width),
        prefetch=1,
        grid=(part_count,),
        in_specs=[
            fixed(tokens, kv_width),
            fixed(1, tokens),
            fixed(*probs.shape),
            fixed(tokens, width),
            late(part_rows, tokens),
            late(part_rows, tokens),
            late(part_rows, width),
            late(part_rows, width),
            fixed(LANES, LANES),
        ],
        out_specs=fixed(LANES, LANES),
        scratch_shapes=[pltpu.VMEM((tokens, width), BF16), pair_total],
    )(flag, values1, mean1, probs, mixed, ct, grad1, out_w, slope, out_part)

    rot_part = call(
        value_part_kernel,
        shaped((count * LANES, LANES), BF16),
        (4 * local * kv_width * tokens, 4 * local * kv_width),
        grid=(1,),
        in_specs=[
            pl.BlockSpec(memory_space=pltpu.SMEM),
            split(local, tokens),
            split(local, tokens),
            whole(1, tokens),
            whole(1, tokens),
            split(local, tokens),
            whole(tokens, kv_width),
            whole(tokens, kv_width),
            split(local, kv_width),
            split(local, kv_width),
            whole(LANES, LANES),
        ],
        out_specs=whole(count * LANES, LANES),
        scratch_shapes=[pltpu.VMEM((LANES, LANES), F32)],
    )(flag, x0, arrived, mean0, mean1, gain, vg0, vg1, value_w, value_slope, out_part)
    rot_grad, rot_new = call(
        cayley_kernel,
        (shaped((LANES, LANES), F32), shaped((LANES, LANES), F32)),
        (12 * 5 * LANES**3, 8 * LANES**2),
    )(exchange(rot_part), rot)
    return rot_grad[None], rot_new[None]


def solution(mesh):
    in_specs = (
        P("groups", "tensor"),
        P("groups", "tensor"),
        P("section", "tensor"),
        P("section", "tensor", None),
        P("section", "tensor", None),
        P("section", None, None),
        P("section", "groups", None, None),
    )
    out_specs = (P("section", "groups", None), P("section", "groups", None))
    return jax.shard_map(
        on_device, mesh=mesh, in_specs=in_specs, out_specs=out_specs, check_vma=False
    )
```

```python
import functools

import jax
import jax.numpy as jnp
from jax import lax
from jax.experimental import pallas as pl
from jax.experimental.pallas import tpu as pltpu
from jax.sharding import PartitionSpec as P

quant_levels = 7.0
norm_eps = 1e-05
scale_eps = 1e-06
step_size = 0.1
precise = lax.Precision.HIGHEST
F32 = jnp.float32
BF16 = jnp.bfloat16
LANES = 128
VMEM_BYTES = 56 * 1024 * 1024

sin_coefs = (3.141582078119497, -5.16714420271071, 2.541908924984016, -0.5546570710297597)
sin_top = sin_coefs[3]
slope_factor = 2.0 * sin_top * sin_top
unit = 1.000002 / (sin_top * sin_top)


def dot_nn(a, b):
    return lax.dot_general(a, b, (((1,), (0,)), ((), ())), preferred_element_type=F32)


def dot_nt(a, b):
    return lax.dot_general(a, b, (((1,), (1,)), ((), ())), preferred_element_type=F32)


def dot_tn(a, b):
    return lax.dot_general(a, b, (((0,), (0,)), ((), ())), preferred_element_type=F32)


def sine_scale(scale):
    return scale * (-sin_top * sin_top / 3.141592653589793)


def soft_parts(turned, inverse, factor):
    ratio = turned * inverse
    rest = ratio - jnp.round(ratio)
    square = rest * rest
    sine = rest * (
        ((square + sin_coefs[2] / sin_top) * square + sin_coefs[1] / sin_top) * square
        + sin_coefs[0] / sin_top
    )
    slope = sine * sine
    below = unit - slope
    return turned - (sine * (below * lax.rsqrt(below))) * factor, slope


def rotation_pair(rot):
    high = rot.astype(BF16)
    low = (rot - high.astype(F32)).astype(BF16)
    zero = jnp.zeros_like(high)

    def blocks(part):
        return jnp.concatenate(
            [jnp.concatenate([part, zero], 1), jnp.concatenate([zero, part], 1)], 0
        )

    return blocks(high), blocks(low)


def column_of(row):
    count = row.shape[1]
    return jnp.transpose(jnp.broadcast_to(row, (count, count)))


def call(kernel, out_shape, cost, **kw):
    flops, moved = cost
    prefetch = kw.pop("prefetch", 0)
    if prefetch:
        names = ("grid", "in_specs", "out_specs", "scratch_shapes")
        fields = {name: kw.pop(name) for name in names if name in kw}
        kw["grid_spec"] = pltpu.PrefetchScalarGridSpec(num_scalar_prefetch=prefetch, **fields)
    return pl.pallas_call(
        kernel,
        out_shape=out_shape,
        compiler_params=pltpu.CompilerParams(vmem_limit_bytes=VMEM_BYTES),
        cost_estimate=pl.CostEstimate(flops=flops, bytes_accessed=moved, transcendentals=0),
        **kw,
    )


def shaped(shape, dtype):
    return jax.ShapeDtypeStruct(shape, dtype)


def value_rot_kernel(
    hidden_ref, ct_ref, gain_row_ref, value_ref, rot_ref,
    x_ref, ct_t_ref, gain_ref, vrot_ref, stats_ref, stat_ref,
):
    kv_width = value_ref.shape[1]
    high, low = rotation_pair(rot_ref[...])

    @pl.when(pl.program_id(0) == 0)
    def _():
        stat_ref[...] = jnp.zeros_like(stat_ref)

    for at in range(0, kv_width, 2 * LANES):
        cols = slice(at, at + 2 * LANES)
        block = value_ref[:, cols]
        turned = dot_nn(block, high) + dot_nn(block, low)
        vrot_ref[:, cols] = turned
        peak = jnp.max(jnp.abs(turned), axis=0, keepdims=True)
        stat_ref[:, cols] = jnp.maximum(stat_ref[:, cols], peak)
    x = jnp.transpose(hidden_ref[...].astype(F32))
    x_ref[...] = x.astype(BF16)
    stat_ref[:, kv_width:] += jnp.sum(x * x, axis=0, keepdims=True)
    ct_t_ref[...] = jnp.transpose(ct_ref[...].astype(F32)).astype(BF16)
    gain_ref[...] = jnp.transpose(jnp.broadcast_to(gain_row_ref[...], hidden_ref.shape))

    @pl.when(pl.program_id(0) == pl.num_programs(0) - 1)
    def _():
        stats_ref[...] = jnp.broadcast_to(stat_ref[...], stats_ref.shape)


def mix_back(probs_ref, grad_of, out_ref, seq, per_group, kv_count):
    blocks = probs_ref.shape[0]
    for b in range(blocks):
        rows = slice(b * seq, (b + 1) * seq)
        for k in range(kv_count):
            stacked = jnp.concatenate(
                [
                    grad_of(rows, slice(h * LANES, (h + 1) * LANES))
                    for h in range(k * per_group, (k + 1) * per_group)
                ],
                0,
            )
            probs = probs_ref[b, k * per_group * seq : (k + 1) * per_group * seq, :]
            out_ref[rows, k * LANES : (k + 1) * LANES] = dot_tn(probs, stacked).astype(
                out_ref.dtype
            )


def mix_forward(probs_ref, values_of, mixed_ref, seq, per_group, kv_count):
    blocks = probs_ref.shape[0]
    for b in range(blocks):
        rows = slice(b * seq, (b + 1) * seq)
        for k in range(kv_count):
            probs = probs_ref[b, k * per_group * seq : (k + 1) * per_group * seq, :]
            heads = dot_nn(probs, values_of(rows, slice(k * LANES, (k + 1) * LANES))).astype(BF16)
            for j in range(per_group):
                h = k * per_group + j
                mixed_ref[rows, h * LANES : (h + 1) * LANES] = heads[j * seq : (j + 1) * seq]


def prep_kernel(kv_count, starts, ends, number, *refs):
    refs = list(refs)
    w_ref, rot_ref, ct_ref = refs[:3]
    del refs[:3]
    if ends:
        probs_ref = refs.pop(0)
    if not starts:
        held_ref = refs[1]
        del refs[:4]
    q_ref, slope_ref = refs[:2]
    del refs[:2]
    back_ref = refs.pop(0)
    if ends:
        vg_ref = refs.pop(0)
    total_ref, turned_ref, inv_ref, factor_ref = refs
    rows, width = w_ref.shape
    step, last = pl.program_id(0), number - 1
    lines = 16
    wide = min(1024, width)

    @pl.when(step == 0)
    def _():
        total_ref[...] = jnp.zeros_like(total_ref)

    high, low = rotation_pair(rot_ref[...])
    peak = jnp.zeros((rows, LANES), F32)
    for at in range(0, width, 2 * LANES):
        cols = slice(at, at + 2 * LANES)
        block = w_ref[:, cols]
        turned = dot_nn(block, high) + dot_nn(block, low)
        turned_ref[:, cols] = turned
        size = jnp.abs(turned)
        peak = jnp.maximum(peak, jnp.maximum(size[:, :LANES], size[:, LANES:]))
    scale = (jnp.max(peak, axis=1, keepdims=True) + scale_eps) / quant_levels
    inv_ref[...] = jnp.broadcast_to(1.0 / scale, inv_ref.shape)
    factor_ref[...] = jnp.broadcast_to(sine_scale(scale), inv_ref.shape)

    @pl.loop(0, rows // lines, unroll=2)
    def _(i):
        here = pl.ds(pl.multiple_of(i * lines, lines), lines)
        inverse, factor = inv_ref[here, :], factor_ref[here, :]
        for at in range(0, width, LANES):
            cols = slice(at, at + LANES)
            effective, slope = soft_parts(turned_ref[here, cols], inverse, factor)
            q_ref[here, cols] = effective.astype(BF16)
            slope_ref[here, cols] = slope.astype(BF16)

    for at in range(0, width, wide):
        cols = slice(at, at + wide)
        total_ref[:, cols] += dot_tn(ct_ref[...], q_ref[:, cols])

    if ends:

        @pl.when(step == last)
        def _():
            if not starts:
                total_ref[...] += held_ref[...].astype(F32)
            back_ref[...] = total_ref[...].astype(BF16)
            seq = probs_ref.shape[2]
            per_group = width // LANES // kv_count
            mix_back(probs_ref, lambda r, c: back_ref[r, c], vg_ref, seq, per_group, kv_count)
    else:

        @pl.when(step == last)
        def _():
            back_ref[...] = total_ref[...].astype(BF16)


def value_quant_kernel(
    model_width, turned_ref, stats_ref, x_ref, gain_ref, q_ref, slope_ref, part_ref, mean_ref, total_ref
):
    kv_width = turned_ref.shape[1]
    stats = stats_ref[...]
    scale = (jnp.max(stats[:, :kv_width], axis=0, keepdims=True) + scale_eps) / quant_levels
    squares = jnp.sum(stats[:, kv_width:], axis=0, keepdims=True)
    mean = lax.rsqrt(squares / model_width + norm_eps)
    inverse = 1.0 / scale
    factor = sine_scale(scale)
    lines = 16
    inverses = [
        jnp.broadcast_to(inverse[:, at : at + LANES], (lines, LANES))
        for at in range(0, kv_width, LANES)
    ]

    @pl.loop(0, turned_ref.shape[0] // lines)
    def _(i):
        here = pl.ds(pl.multiple_of(i * lines, lines), lines)
        for j, wide in enumerate(inverses):
            cols = slice(j * LANES, (j + 1) * LANES)
            effective, slope = soft_parts(turned_ref[here, cols], wide, factor[:, cols])
            q_ref[here, cols] = effective.astype(BF16)
            slope_ref[here, cols] = slope.astype(BF16)

    @pl.when(pl.program_id(0) == 0)
    def _():
        mean_ref[...] = mean
        total_ref[...] = jnp.zeros_like(total_ref)

    normed = (x_ref[...].astype(F32) * mean * gain_ref[...]).astype(BF16)
    total_ref[...] += dot_tn(normed, q_ref[...])

    @pl.when(pl.program_id(0) == pl.num_programs(0) - 1)
    def _():
        part_ref[...] = total_ref[...].astype(BF16)


def forward_kernel(kv_count, active_ref, values_ref, probs_ref, q_ref, x_ref, mixed_ref, out_ref):
    @pl.when(active_ref[0] == 1)
    def _():
        @pl.when(pl.program_id(0) == 0)
        def _():
            seq = probs_ref.shape[2]
            per_group = q_ref.shape[1] // LANES // kv_count
            mix_forward(
                probs_ref, lambda r, c: values_ref[r, c], mixed_ref, seq, per_group, kv_count
            )

        out_ref[...] = (x_ref[...].astype(F32) + dot_nt(q_ref[...], mixed_ref[...])).astype(BF16)


def back_kernel(active_ref, q_ref, grad_ref, after_ref, back_ref, total_ref):
    width = q_ref.shape[1]

    @pl.when(active_ref[0] == 1)
    def _():
        @pl.when(pl.program_id(0) == 0)
        def _():
            total_ref[...] = jnp.zeros_like(total_ref)

        wide = min(1024, width)
        for at in range(0, width, wide):
            cols = slice(at, at + wide)
            total_ref[:, cols] += dot_tn(grad_ref[...], q_ref[:, cols])

        @pl.when(pl.program_id(0) == pl.num_programs(0) - 1)
        def _():
            back_ref[...] = total_ref[...].astype(BF16)


def project_kernel(
    active_ref, own_ref, arrived_ref, vg_ref, gain_ref, q_ref, out_ref, grad_ref, total_ref, sum_ref
):
    kv_width = q_ref.shape[1]
    last_section = active_ref[0] == 1
    first, last = pl.program_id(0) == 0, pl.program_id(0) == pl.num_programs(0) - 1

    @pl.when(first)
    def _():
        total_ref[...] = jnp.zeros_like(total_ref)
        sum_ref[...] = jnp.zeros_like(sum_ref)

    x = jnp.where(last_section, arrived_ref[...], own_ref[...]).astype(F32)
    sum_ref[...] += jnp.sum(x * x, axis=0, keepdims=True)

    @pl.when(last_section)
    def _():
        total_ref[...] += dot_tn((x * gain_ref[...]).astype(BF16), q_ref[...])
        grad_ref[...] = (dot_nt(q_ref[...], vg_ref[...]) * gain_ref[...]).astype(BF16)

    @pl.when(last)
    def _():
        out_ref[:, :kv_width] = total_ref[...].astype(BF16)
        tokens = sum_ref.shape[1]
        out_ref[:, kv_width:] = jnp.broadcast_to(sum_ref[...], (tokens, tokens)).astype(BF16)


def value_grad_kernel(kv_count, active_ref, mean_ref, ct_back_ref, back_ref, probs_ref, out_ref, inv_ref):
    seq = probs_ref.shape[2]
    per_group = back_ref.shape[1] // LANES // kv_count

    @pl.when(active_ref[0] == 1)
    def _():
        inv_ref[...] = column_of(mean_ref[...])
        inverse = inv_ref[pl.ds(pl.multiple_of(pl.program_id(0) * seq, seq), seq), :1]

        def grad_of(rows, cols):
            return (
                ct_back_ref[rows, cols].astype(F32) + inverse * back_ref[rows, cols].astype(F32)
            ).astype(BF16)

        mix_back(probs_ref, grad_of, out_ref, seq, per_group, kv_count)


def out_grad_block(grad, mixed_ref, w_ref, slope_ref, total_ref):
    width, together = w_ref.shape[1], 4
    for first in range(0, width, 2 * LANES * together):
        pieces = []
        for at in range(first, min(first + 2 * LANES * together, width), 2 * LANES):
            cols = slice(at, at + 2 * LANES)
            out_grad = dot_nn(grad, mixed_ref[:, cols])
            sloped = (out_grad * slope_ref[:, cols].astype(F32)).astype(BF16)
            pieces.append((w_ref[:, cols], sloped))
        total_ref[...] += dot_tn(*(jnp.concatenate(side, 0) for side in zip(*pieces)))


def both_heads(total_ref):
    return total_ref[:LANES, :LANES] + total_ref[LANES:, LANES:]


def early_grad_kernel(
    section_ref, mean_ref, mixed_ref, ct_ref, grad_ref, w_ref, slope_ref, after_ref, out_ref, total_ref
):
    @pl.when(pl.program_id(0) == 0)
    def _():
        total_ref[...] = jnp.zeros_like(total_ref)

    @pl.when(section_ref[0] == 0)
    def _():
        grad = (ct_ref[...].astype(F32) + mean_ref[...] * grad_ref[...].astype(F32)).astype(BF16)
        out_grad_block(grad, mixed_ref, w_ref, slope_ref, total_ref)

    @pl.when(pl.program_id(0) == pl.num_programs(0) - 1)
    def _():
        out_ref[...] = both_heads(total_ref)


def out_grad_kernel(
    kv_count, half, section_ref, values_ref, mean_ref, probs_ref, mixed_in_ref,
    ct_ref, grad_ref, w_ref, slope_ref, other_ref, out_ref, mixed_ref, total_ref,
):
    seq = probs_ref.shape[2]
    per_group = w_ref.shape[1] // LANES // kv_count
    last_section = section_ref[0] != 0

    @pl.when(pl.program_id(0) == 0)
    def _():
        total_ref[...] = jnp.zeros_like(total_ref)

        @pl.when(last_section)
        def _():
            mix_forward(
                probs_ref, lambda r, c: values_ref[r, c], mixed_ref, seq, per_group, kv_count
            )

    @pl.when(last_section)
    def _():
        out_grad_block(ct_ref[...], mixed_ref, w_ref, slope_ref, total_ref)

    @pl.when(jnp.logical_and(section_ref[0] == 0, pl.program_id(0) >= half))
    def _():
        grad = (ct_ref[...].astype(F32) + mean_ref[...] * grad_ref[...].astype(F32)).astype(BF16)
        out_grad_block(grad, mixed_in_ref, w_ref, slope_ref, total_ref)

    @pl.when(pl.program_id(0) == pl.num_programs(0) - 1)
    def _():
        out_ref[...] = both_heads(total_ref)
        if half:
            out_ref[...] += other_ref[...]


def value_part_kernel(
    section_ref, x0_ref, x1_ref, mean0_ref, mean1_ref, gain_ref, vg0_ref, vg1_ref, v_ref, slope_ref,
    other_ref, out_ref, total_ref,
):
    first = section_ref[0] == 0
    x = jnp.where(first, x0_ref[...], x1_ref[...]).astype(F32)
    mean = jnp.where(first, mean0_ref[...], mean1_ref[...])
    normed = (x * mean * gain_ref[...]).astype(BF16)

    @pl.when(pl.program_id(0) == 0)
    def _():
        total_ref[...] = other_ref[...]

    pieces = []
    for at in range(0, v_ref.shape[1], 2 * LANES):
        cols = slice(at, at + 2 * LANES)
        grad = dot_nn(normed, jnp.where(first, vg0_ref[:, cols], vg1_ref[:, cols]))
        sloped = (grad * slope_ref[:, cols].astype(F32)).astype(BF16)
        pieces.append((v_ref[:, cols], sloped))
    both = dot_tn(*(jnp.concatenate(side, 0) for side in zip(*pieces)))
    total_ref[...] += both[:LANES, :LANES] + both[LANES:, LANES:]

    @pl.when(pl.program_id(0) == pl.num_programs(0) - 1)
    def _():
        total = (slope_factor * total_ref[...]).astype(out_ref.dtype)
        for i in range(out_ref.shape[0] // LANES):
            out_ref[i * LANES : (i + 1) * LANES] = total


def cayley_kernel(parts_ref, rot_ref, grad_ref, new_ref):
    count = parts_ref.shape[0] // LANES
    grad = parts_ref[:LANES].astype(F32)
    for i in range(1, count):
        grad = grad + parts_ref[i * LANES : (i + 1) * LANES].astype(F32)
    grad_ref[...] = grad
    rot = rot_ref[...]

    def product(a, b, dims=(1, 0)):
        return lax.dot_general(
            a, b, (((dims[0],), (dims[1],)), ((), ())), precision=precise, preferred_element_type=F32
        )

    turn = product(grad, rot, (1, 1))
    skew = turn - jnp.transpose(turn)
    update = rot - step_size * product(skew, rot)
    for _ in range(2):
        update = rot - 0.5 * step_size * product(skew, rot + update)
    new_ref[...] = update


def exchange(rows):
    return lax.all_to_all(rows, "tensor", split_axis=0, concat_axis=0, tiled=True)


def on_device(hidden, cotangent, norm_gain, value_weight, output_weight, rotation, attention):
    section = lax.axis_index("section")
    count = lax.axis_size("tensor")
    is_first = section == 0
    flag = section.astype(jnp.int32).reshape(1)
    rot = rotation[0]
    value_w = value_weight[0]
    out_w = output_weight[0]
    local, width = out_w.shape
    kv_width = value_w.shape[1]
    kv_count = kv_width // LANES
    tokens = hidden.shape[0]
    _, blocks, heads, flat = attention.shape
    seq = tokens // blocks
    probs = attention[0].reshape(blocks, heads * seq, seq)
    model_width = local * count
    big = 2 * tokens * local * width

    def split(rows, *tail):
        return pl.BlockSpec((rows,) + tail, lambda i: (i, 0))

    def across(lines, rows):
        return pl.BlockSpec((lines, rows), lambda i: (0, i))

    def whole(*shape):
        return pl.BlockSpec(shape, lambda i: (0,) * len(shape))

    rows = min(local, 256)
    half_rows = max(local // 2, min(local, 128))
    x0, ct, gain, value_rot, stat = call(
        value_rot_kernel,
        (
            shaped((local, tokens), BF16),
            shaped((local, tokens), BF16),
            shaped((local, tokens), F32),
            shaped((local, kv_width), F32),
            shaped((count, kv_width + tokens), F32),
        ),
        (4 * local * kv_width * LANES, 6 * local * kv_width),
        grid=(local // half_rows,),
        in_specs=[
            across(tokens, half_rows),
            across(tokens, half_rows),
            across(1, half_rows),
            split(half_rows, kv_width),
            whole(LANES, LANES),
        ],
        out_specs=(
            split(half_rows, tokens),
            split(half_rows, tokens),
            split(half_rows, tokens),
            split(half_rows, kv_width),
            whole(count, kv_width + tokens),
        ),
        scratch_shapes=[pltpu.VMEM((1, kv_width + tokens), F32)],
    )(hidden, cotangent, norm_gain, value_w, rot)
    stats = exchange(stat)

    part_rows = min(local, 128)
    part_count = local // part_rows

    def prepare(first, number, before):
        starts, ends = first == 0, first + number == part_count

        def ahead(lines, *tail):
            return pl.BlockSpec((lines,) + tail, lambda i: (first + i, 0))

        def behind(lines, *tail):
            return pl.BlockSpec((lines,) + tail, lambda i: (first + i, 0))

        anywhere = pl.BlockSpec(memory_space=pl.ANY)
        operands = [out_w, rot, ct]
        in_specs = [ahead(part_rows, width), whole(LANES, LANES), behind(part_rows, tokens)]
        if ends:
            operands.append(probs)
            in_specs.append(whole(*probs.shape))
        aliases = {}
        if not starts:
            quant, slope, held, after = before
            at = len(operands)
            operands += [after, held, quant, slope]
            in_specs += [anywhere, whole(tokens, width), anywhere, anywhere]
            aliases = {at + 2: 0, at + 3: 1}
        outs = [shaped((local, width), BF16), shaped((local, width), BF16)]
        out_specs = [behind(part_rows, width), behind(part_rows, width)]
        scratch = [pltpu.VMEM((tokens, width), F32)]
        if ends:
            outs += [shaped((tokens, width), BF16), shaped((tokens, kv_width), BF16)]
            out_specs += [whole(tokens, width), whole(tokens, kv_width)]
        else:
            outs.append(shaped((tokens, width), BF16))
            out_specs.append(whole(tokens, width))
        scratch += [
            pltpu.VMEM((part_rows, width), F32),
            pltpu.VMEM((part_rows, LANES), F32),
            pltpu.VMEM((part_rows, LANES), F32),
        ]
        return call(
            functools.partial(prep_kernel, kv_count, starts, ends, number),
            tuple(outs),
            (40 * big * number // part_count, 6 * local * width * number // part_count),
            grid=(number,),
            in_specs=in_specs,
            out_specs=tuple(out_specs),
            scratch_shapes=scratch,
            input_output_aliases=aliases,
        )(*operands)

    lead = part_count // 4
    before = prepare(0, lead, None) if lead else None

    value_q, value_slope, value_part, mean0 = call(
        functools.partial(value_quant_kernel, model_width),
        (
            shaped((local, kv_width), BF16),
            shaped((local, kv_width), BF16),
            shaped((tokens, kv_width), BF16),
            shaped((1, tokens), F32),
        ),
        (2 * local * kv_width * tokens, 8 * local * kv_width),
        grid=(local // half_rows,),
        in_specs=[
            split(half_rows, kv_width),
            whole(count, kv_width + tokens),
            split(half_rows, tokens),
            split(half_rows, tokens),
        ],
        out_specs=(
            split(half_rows, kv_width),
            split(half_rows, kv_width),
            whole(tokens, kv_width),
            whole(1, tokens),
        ),
        scratch_shapes=[pltpu.VMEM((tokens, kv_width), F32)],
    )(value_rot, stats, x0, gain)

    def add_parts(received):
        return received.reshape(count, tokens // count, -1).astype(F32).sum(0)

    def spread(part):
        return jnp.tile(part.astype(BF16), (count, 1))

    values0 = spread(add_parts(exchange(value_part)))
    if lead:
        before = tuple(before) + (value_part,)
    quant, slope, ct_back, ct_vg = prepare(lead, part_count - lead, before)

    on_first = 1 - flag
    anywhere = pl.BlockSpec(memory_space=pl.ANY)

    def only(lines, *tail):
        return pl.BlockSpec((lines,) + tail, lambda i, active: (i * active[0], 0))

    def each(lines, *tail):
        return pl.BlockSpec((lines,) + tail, lambda i, active: (i, 0))

    def fixed(*shape):
        return pl.BlockSpec(shape, lambda i, active: (0,) * len(shape))

    second = exchange(jnp.where(is_first, values0, ct_vg))
    second, to_gather = lax.optimization_barrier((second, spread(add_parts(second))))
    vg1 = exchange(to_gather)

    mixed, x1 = call(
        functools.partial(forward_kernel, kv_count),
        (shaped((tokens, width), BF16), shaped((local, tokens), BF16)),
        (big, 2 * local * width),
        prefetch=1,
        grid=(local // rows,),
        in_specs=[
            fixed(tokens, kv_width),
            fixed(*probs.shape),
            only(rows, width),
            only(rows, tokens),
        ],
        out_specs=(fixed(tokens, width), only(rows, tokens)),
    )(on_first, second, probs, quant, x0)
    arrived = lax.ppermute(x1, "section", [(0, 1)])

    projected, grad1 = call(
        project_kernel,
        (shaped((tokens, kv_width + tokens), BF16), shaped((local, tokens), BF16)),
        (4 * local * kv_width * tokens, 2 * local * kv_width),
        prefetch=1,
        grid=(local // half_rows,),
        in_specs=[
            each(half_rows, tokens),
            each(half_rows, tokens),
            fixed(tokens, kv_width),
            each(half_rows, tokens),
            only(half_rows, kv_width),
        ],
        out_specs=(fixed(tokens, kv_width + tokens), only(half_rows, tokens)),
        scratch_shapes=[pltpu.VMEM((tokens, kv_width), F32), pltpu.VMEM((1, tokens), F32)],
    )(flag, x1, arrived, vg1, gain, value_q)
    received = add_parts(exchange(projected))
    mean1 = lax.rsqrt(received[:1, kv_width:] / model_width + norm_eps)

    grad1 = lax.ppermute(grad1, "section", [(1, 0)])
    grad_back = call(
        back_kernel,
        shaped((tokens, width), BF16),
        (big, 2 * local * width),
        prefetch=1,
        grid=(local // rows,),
        in_specs=[only(rows, width), only(rows, tokens), anywhere],
        out_specs=fixed(tokens, width),
        scratch_shapes=[pltpu.VMEM((tokens, width), F32)],
    )(on_first, quant, grad1, projected)

    vg0 = call(
        functools.partial(value_grad_kernel, kv_count),
        shaped((tokens, kv_width), BF16),
        (2 * tokens * width * seq, 6 * tokens * width),
        prefetch=1,
        grid=(blocks,),
        in_specs=[
            fixed(1, tokens),
            each(seq, width),
            each(seq, width),
            pl.BlockSpec((1, heads * seq, seq), lambda i, active: (i, 0, 0)),
        ],
        out_specs=each(seq, kv_width),
        scratch_shapes=[pltpu.VMEM((tokens, tokens), F32)],
    )(on_first, mean1, ct_back, grad_back, probs)
    mine = lax.axis_index("tensor") * (tokens // count)
    own_mean = lax.dynamic_slice(mean1[0], (mine,), (tokens // count,))[:, None]
    to_send = jnp.where(is_first, vg0, spread(received[:, :kv_width] * own_mean))
    values1 = exchange(to_send)

    def early(lines, *tail):
        return pl.BlockSpec((lines,) + tail, lambda i, section: (i * (1 - section[0]), 0))

    half = local // rows // 2
    pair_total = pltpu.VMEM((2 * LANES, 2 * LANES), F32)
    out_part = jnp.zeros((LANES, LANES), F32)
    if half:
        out_part = call(
            early_grad_kernel,
            shaped((LANES, LANES), F32),
            (big, 2 * local * width),
            prefetch=1,
            grid=(half,),
            in_specs=[
                fixed(1, tokens),
                fixed(tokens, width),
                early(rows, tokens),
                early(rows, tokens),
                early(rows, width),
                early(rows, width),
                anywhere,
            ],
            out_specs=fixed(LANES, LANES),
            scratch_shapes=[pair_total],
        )(flag, mean1, mixed, ct, grad1, out_w, slope, to_send)
        values1, out_part = lax.optimization_barrier((values1, out_part))
    vg0 = exchange(spread(add_parts(values1)))

    def late(lines, *tail):
        return pl.BlockSpec(
            (lines,) + tail, lambda i, section: (jnp.maximum(i, (1 - section[0]) * half), 0)
        )

    out_part = call(
        functools.partial(out_grad_kernel, kv_count, half),
        shaped((LANES, LANES), F32),
        (2 * big, 4 * local * width),
        prefetch=1,
        grid=(local // rows,),
        in_specs=[
            fixed(tokens, kv_width),
            fixed(1, tokens),
            fixed(*probs.shape),
            fixed(tokens, width),
            late(rows, tokens),
            late(rows, tokens),
            late(rows, width),
            late(rows, width),
            fixed(LANES, LANES),
        ],
        out_specs=fixed(LANES, LANES),
        scratch_shapes=[pltpu.VMEM((tokens, width), BF16), pair_total],
    )(flag, values1, mean1, probs, mixed, ct, grad1, out_w, slope, out_part)

    rot_part = call(
        value_part_kernel,
        shaped((count * LANES, LANES), BF16),
        (4 * local * kv_width * tokens, 4 * local * kv_width),
        grid=(1,),
        in_specs=[
            pl.BlockSpec(memory_space=pltpu.SMEM),
            split(local, tokens),
            split(local, tokens),
            whole(1, tokens),
            whole(1, tokens),
            split(local, tokens),
            whole(tokens, kv_width),
            whole(tokens, kv_width),
            split(local, kv_width),
            split(local, kv_width),
            whole(LANES, LANES),
        ],
        out_specs=whole(count * LANES, LANES),
        scratch_shapes=[pltpu.VMEM((LANES, LANES), F32)],
    )(flag, x0, arrived, mean0, mean1, gain, vg0, vg1, value_w, value_slope, out_part)
    rot_grad, rot_new = call(
        cayley_kernel,
        (shaped((LANES, LANES), F32), shaped((LANES, LANES), F32)),
        (12 * 5 * LANES**3, 8 * LANES**2),
    )(exchange(rot_part), rot)
    return rot_grad[None], rot_new[None]


def solution(mesh):
    in_specs = (
        P("groups", "tensor"),
        P("groups", "tensor"),
        P("section", "tensor"),
        P("section", "tensor", None),
        P("section", "tensor", None),
        P("section", None, None),
        P("section", "groups", None, None),
    )
    out_specs = (P("section", "groups", None), P("section", "groups", None))
    return jax.shard_map(
        on_device, mesh=mesh, in_specs=in_specs, out_specs=out_specs, check_vma=False
    )
```

```python
import functools

import jax
import jax.numpy as jnp
from jax import lax
from jax.experimental import pallas as pl
from jax.experimental.pallas import tpu as pltpu
from jax.sharding import PartitionSpec as P

quant_levels = 7.0
norm_eps = 1e-05
scale_eps = 1e-06
step_size = 0.1
precise = lax.Precision.HIGHEST
F32 = jnp.float32
BF16 = jnp.bfloat16
LANES = 128
VMEM_BYTES = 56 * 1024 * 1024

sin_coefs = (3.141582078119497, -5.16714420271071, 2.541908924984016, -0.5546570710297597)
sin_top = sin_coefs[3]
slope_factor = 2.0 * sin_top * sin_top
unit = 1.000002 / (sin_top * sin_top)


def dot_nn(a, b):
    return lax.dot_general(a, b, (((1,), (0,)), ((), ())), preferred_element_type=F32)


def dot_nt(a, b):
    return lax.dot_general(a, b, (((1,), (1,)), ((), ())), preferred_element_type=F32)


def dot_tn(a, b):
    return lax.dot_general(a, b, (((0,), (0,)), ((), ())), preferred_element_type=F32)


def sine_scale(scale):
    return scale * (-sin_top * sin_top / 3.141592653589793)


def soft_parts(turned, inverse, factor):
    ratio = turned * inverse
    rest = ratio - jnp.round(ratio)
    square = rest * rest
    sine = rest * (
        ((square + sin_coefs[2] / sin_top) * square + sin_coefs[1] / sin_top) * square
        + sin_coefs[0] / sin_top
    )
    slope = sine * sine
    below = unit - slope
    return turned - (sine * (below * lax.rsqrt(below))) * factor, slope


def rotation_pair(rot):
    high = rot.astype(BF16)
    low = (rot - high.astype(F32)).astype(BF16)
    zero = jnp.zeros_like(high)

    def blocks(part):
        return jnp.concatenate(
            [jnp.concatenate([part, zero], 1), jnp.concatenate([zero, part], 1)], 0
        )

    return blocks(high), blocks(low)


def column_of(row):
    count = row.shape[1]
    return jnp.transpose(jnp.broadcast_to(row, (count, count)))


def call(kernel, out_shape, cost, **kw):
    flops, moved = cost
    prefetch = kw.pop("prefetch", 0)
    if prefetch:
        names = ("grid", "in_specs", "out_specs", "scratch_shapes")
        fields = {name: kw.pop(name) for name in names if name in kw}
        kw["grid_spec"] = pltpu.PrefetchScalarGridSpec(num_scalar_prefetch=prefetch, **fields)
    return pl.pallas_call(
        kernel,
        out_shape=out_shape,
        compiler_params=pltpu.CompilerParams(vmem_limit_bytes=VMEM_BYTES),
        cost_estimate=pl.CostEstimate(flops=flops, bytes_accessed=moved, transcendentals=0),
        **kw,
    )


def shaped(shape, dtype):
    return jax.ShapeDtypeStruct(shape, dtype)


def value_rot_kernel(
    hidden_ref, ct_ref, gain_row_ref, value_ref, rot_ref,
    x_ref, ct_t_ref, gain_ref, vrot_ref, stats_ref, stat_ref,
):
    kv_width = value_ref.shape[1]
    high, low = rotation_pair(rot_ref[...])

    @pl.when(pl.program_id(0) == 0)
    def _():
        stat_ref[...] = jnp.zeros_like(stat_ref)

    for at in range(0, kv_width, 2 * LANES):
        cols = slice(at, at + 2 * LANES)
        block = value_ref[:, cols]
        turned = dot_nn(block, high) + dot_nn(block, low)
        vrot_ref[:, cols] = turned
        peak = jnp.max(jnp.abs(turned), axis=0, keepdims=True)
        stat_ref[:, cols] = jnp.maximum(stat_ref[:, cols], peak)
    x = jnp.transpose(hidden_ref[...].astype(F32))
    x_ref[...] = x.astype(BF16)
    stat_ref[:, kv_width:] += jnp.sum(x * x, axis=0, keepdims=True)
    ct_t_ref[...] = jnp.transpose(ct_ref[...].astype(F32)).astype(BF16)
    gain_ref[...] = jnp.transpose(jnp.broadcast_to(gain_row_ref[...], hidden_ref.shape))

    @pl.when(pl.program_id(0) == pl.num_programs(0) - 1)
    def _():
        stats_ref[...] = jnp.broadcast_to(stat_ref[...], stats_ref.shape)


def mix_back(probs_ref, grad_of, out_ref, seq, per_group, kv_count):
    blocks = probs_ref.shape[0]
    for b in range(blocks):
        rows = slice(b * seq, (b + 1) * seq)
        for k in range(kv_count):
            stacked = jnp.concatenate(
                [
                    grad_of(rows, slice(h * LANES, (h + 1) * LANES))
                    for h in range(k * per_group, (k + 1) * per_group)
                ],
                0,
            )
            probs = probs_ref[b, k * per_group * seq : (k + 1) * per_group * seq, :]
            out_ref[rows, k * LANES : (k + 1) * LANES] = dot_tn(probs, stacked).astype(
                out_ref.dtype
            )


def mix_forward(probs_ref, values_of, mixed_ref, seq, per_group, kv_count):
    blocks = probs_ref.shape[0]
    for b in range(blocks):
        rows = slice(b * seq, (b + 1) * seq)
        for k in range(kv_count):
            probs = probs_ref[b, k * per_group * seq : (k + 1) * per_group * seq, :]
            heads = dot_nn(probs, values_of(rows, slice(k * LANES, (k + 1) * LANES))).astype(BF16)
            for j in range(per_group):
                h = k * per_group + j
                mixed_ref[rows, h * LANES : (h + 1) * LANES] = heads[j * seq : (j + 1) * seq]


def prep_kernel(kv_count, starts, ends, number, *refs):
    refs = list(refs)
    w_ref, rot_ref, ct_ref = refs[:3]
    del refs[:3]
    if ends:
        probs_ref = refs.pop(0)
    if not starts:
        held_ref = refs[1]
        del refs[:4]
    q_ref, slope_ref = refs[:2]
    del refs[:2]
    back_ref = refs.pop(0)
    if ends:
        vg_ref = refs.pop(0)
    total_ref, turned_ref, inv_ref, factor_ref = refs
    rows, width = w_ref.shape
    step, last = pl.program_id(0), number - 1
    lines = 16
    wide = min(1024, width)

    @pl.when(step == 0)
    def _():
        total_ref[...] = jnp.zeros_like(total_ref)

    high, low = rotation_pair(rot_ref[...])
    peak = jnp.zeros((rows, LANES), F32)
    for at in range(0, width, 2 * LANES):
        cols = slice(at, at + 2 * LANES)
        block = w_ref[:, cols]
        turned = dot_nn(block, high) + dot_nn(block, low)
        turned_ref[:, cols] = turned
        size = jnp.abs(turned)
        peak = jnp.maximum(peak, jnp.maximum(size[:, :LANES], size[:, LANES:]))
    scale = (jnp.max(peak, axis=1, keepdims=True) + scale_eps) / quant_levels
    inv_ref[...] = jnp.broadcast_to(1.0 / scale, inv_ref.shape)
    factor_ref[...] = jnp.broadcast_to(sine_scale(scale), inv_ref.shape)

    @pl.loop(0, rows // lines, unroll=2)
    def _(i):
        here = pl.ds(pl.multiple_of(i * lines, lines), lines)
        inverse, factor = inv_ref[here, :], factor_ref[here, :]
        for at in range(0, width, LANES):
            cols = slice(at, at + LANES)
            effective, slope = soft_parts(turned_ref[here, cols], inverse, factor)
            q_ref[here, cols] = effective.astype(BF16)
            slope_ref[here, cols] = slope.astype(BF16)

    for at in range(0, width, wide):
        cols = slice(at, at + wide)
        total_ref[:, cols] += dot_tn(ct_ref[...], q_ref[:, cols])

    if ends:

        @pl.when(step == last)
        def _():
            if not starts:
                total_ref[...] += held_ref[...].astype(F32)
            back_ref[...] = total_ref[...].astype(BF16)
            seq = probs_ref.shape[2]
            per_group = width // LANES // kv_count
            mix_back(probs_ref, lambda r, c: back_ref[r, c], vg_ref, seq, per_group, kv_count)
    else:

        @pl.when(step == last)
        def _():
            back_ref[...] = total_ref[...].astype(BF16)


def value_quant_kernel(
    model_width, turned_ref, stats_ref, x_ref, gain_ref, q_ref, slope_ref, part_ref, mean_ref, total_ref
):
    kv_width = turned_ref.shape[1]
    stats = stats_ref[...]
    scale = (jnp.max(stats[:, :kv_width], axis=0, keepdims=True) + scale_eps) / quant_levels
    squares = jnp.sum(stats[:, kv_width:], axis=0, keepdims=True)
    mean = lax.rsqrt(squares / model_width + norm_eps)
    inverse = 1.0 / scale
    factor = sine_scale(scale)
    lines = 16
    inverses = [
        jnp.broadcast_to(inverse[:, at : at + LANES], (lines, LANES))
        for at in range(0, kv_width, LANES)
    ]

    @pl.loop(0, turned_ref.shape[0] // lines)
    def _(i):
        here = pl.ds(pl.multiple_of(i * lines, lines), lines)
        for j, wide in enumerate(inverses):
            cols = slice(j * LANES, (j + 1) * LANES)
            effective, slope = soft_parts(turned_ref[here, cols], wide, factor[:, cols])
            q_ref[here, cols] = effective.astype(BF16)
            slope_ref[here, cols] = slope.astype(BF16)

    @pl.when(pl.program_id(0) == 0)
    def _():
        mean_ref[...] = mean
        total_ref[...] = jnp.zeros_like(total_ref)

    normed = (x_ref[...].astype(F32) * mean * gain_ref[...]).astype(BF16)
    total_ref[...] += dot_tn(normed, q_ref[...])

    @pl.when(pl.program_id(0) == pl.num_programs(0) - 1)
    def _():
        part_ref[...] = total_ref[...].astype(BF16)


def forward_kernel(kv_count, active_ref, values_ref, probs_ref, q_ref, x_ref, mixed_ref, out_ref):
    @pl.when(active_ref[0] == 1)
    def _():
        @pl.when(pl.program_id(0) == 0)
        def _():
            seq = probs_ref.shape[2]
            per_group = q_ref.shape[1] // LANES // kv_count
            mix_forward(
                probs_ref, lambda r, c: values_ref[r, c], mixed_ref, seq, per_group, kv_count
            )

        out_ref[...] = (x_ref[...].astype(F32) + dot_nt(q_ref[...], mixed_ref[...])).astype(BF16)


def back_kernel(active_ref, q_ref, grad_ref, after_ref, back_ref, total_ref):
    width = q_ref.shape[1]

    @pl.when(active_ref[0] == 1)
    def _():
        @pl.when(pl.program_id(0) == 0)
        def _():
            total_ref[...] = jnp.zeros_like(total_ref)

        wide = min(1024, width)
        for at in range(0, width, wide):
            cols = slice(at, at + wide)
            total_ref[:, cols] += dot_tn(grad_ref[...], q_ref[:, cols])

        @pl.when(pl.program_id(0) == pl.num_programs(0) - 1)
        def _():
            back_ref[...] = total_ref[...].astype(BF16)


def project_kernel(
    active_ref, own_ref, arrived_ref, vg_ref, gain_ref, q_ref, out_ref, grad_ref, total_ref, sum_ref
):
    kv_width = q_ref.shape[1]
    last_section = active_ref[0] == 1
    first, last = pl.program_id(0) == 0, pl.program_id(0) == pl.num_programs(0) - 1

    @pl.when(first)
    def _():
        total_ref[...] = jnp.zeros_like(total_ref)
        sum_ref[...] = jnp.zeros_like(sum_ref)

    x = jnp.where(last_section, arrived_ref[...], own_ref[...]).astype(F32)
    sum_ref[...] += jnp.sum(x * x, axis=0, keepdims=True)

    @pl.when(last_section)
    def _():
        total_ref[...] += dot_tn((x * gain_ref[...]).astype(BF16), q_ref[...])
        grad_ref[...] = (dot_nt(q_ref[...], vg_ref[...]) * gain_ref[...]).astype(BF16)

    @pl.when(last)
    def _():
        out_ref[:, :kv_width] = total_ref[...].astype(BF16)
        tokens = sum_ref.shape[1]
        out_ref[:, kv_width:] = jnp.broadcast_to(sum_ref[...], (tokens, tokens)).astype(BF16)


def value_grad_kernel(kv_count, active_ref, mean_ref, ct_back_ref, back_ref, probs_ref, out_ref, inv_ref):
    seq = probs_ref.shape[2]
    per_group = back_ref.shape[1] // LANES // kv_count

    @pl.when(active_ref[0] == 1)
    def _():
        inv_ref[...] = column_of(mean_ref[...])
        inverse = inv_ref[pl.ds(pl.multiple_of(pl.program_id(0) * seq, seq), seq), :1]

        def grad_of(rows, cols):
            return (
                ct_back_ref[rows, cols].astype(F32) + inverse * back_ref[rows, cols].astype(F32)
            ).astype(BF16)

        mix_back(probs_ref, grad_of, out_ref, seq, per_group, kv_count)


def out_grad_block(grad, mixed_ref, w_ref, slope_ref, total_ref):
    width, together = w_ref.shape[1], 4
    for first in range(0, width, 2 * LANES * together):
        pieces = []
        for at in range(first, min(first + 2 * LANES * together, width), 2 * LANES):
            cols = slice(at, at + 2 * LANES)
            out_grad = dot_nn(grad, mixed_ref[:, cols])
            sloped = (out_grad * slope_ref[:, cols].astype(F32)).astype(BF16)
            pieces.append((w_ref[:, cols], sloped))
        total_ref[...] += dot_tn(*(jnp.concatenate(side, 0) for side in zip(*pieces)))


def both_heads(total_ref):
    return total_ref[:LANES, :LANES] + total_ref[LANES:, LANES:]


def early_grad_kernel(
    section_ref, mean_ref, mixed_ref, ct_ref, grad_ref, w_ref, slope_ref, after_ref, out_ref, total_ref
):
    @pl.when(pl.program_id(0) == 0)
    def _():
        total_ref[...] = jnp.zeros_like(total_ref)

    @pl.when(section_ref[0] == 0)
    def _():
        grad = (ct_ref[...].astype(F32) + mean_ref[...] * grad_ref[...].astype(F32)).astype(BF16)
        out_grad_block(grad, mixed_ref, w_ref, slope_ref, total_ref)

    @pl.when(pl.program_id(0) == pl.num_programs(0) - 1)
    def _():
        out_ref[...] = both_heads(total_ref)


def out_grad_kernel(
    kv_count, half, section_ref, values_ref, mean_ref, probs_ref, mixed_in_ref,
    ct_ref, grad_ref, w_ref, slope_ref, other_ref, out_ref, mixed_ref, total_ref,
):
    seq = probs_ref.shape[2]
    per_group = w_ref.shape[1] // LANES // kv_count
    last_section = section_ref[0] != 0

    @pl.when(pl.program_id(0) == 0)
    def _():
        total_ref[...] = jnp.zeros_like(total_ref)

        @pl.when(last_section)
        def _():
            mix_forward(
                probs_ref, lambda r, c: values_ref[r, c], mixed_ref, seq, per_group, kv_count
            )

    @pl.when(last_section)
    def _():
        out_grad_block(ct_ref[...], mixed_ref, w_ref, slope_ref, total_ref)

    @pl.when(jnp.logical_and(section_ref[0] == 0, pl.program_id(0) >= half))
    def _():
        grad = (ct_ref[...].astype(F32) + mean_ref[...] * grad_ref[...].astype(F32)).astype(BF16)
        out_grad_block(grad, mixed_in_ref, w_ref, slope_ref, total_ref)

    @pl.when(pl.program_id(0) == pl.num_programs(0) - 1)
    def _():
        out_ref[...] = both_heads(total_ref)
        if half:
            out_ref[...] += other_ref[...]


def value_part_kernel(
    section_ref, x0_ref, x1_ref, mean0_ref, mean1_ref, gain_ref, vg0_ref, vg1_ref, v_ref, slope_ref,
    other_ref, out_ref, total_ref,
):
    first = section_ref[0] == 0
    x = jnp.where(first, x0_ref[...], x1_ref[...]).astype(F32)
    mean = jnp.where(first, mean0_ref[...], mean1_ref[...])
    normed = (x * mean * gain_ref[...]).astype(BF16)

    @pl.when(pl.program_id(0) == 0)
    def _():
        total_ref[...] = other_ref[...]

    pieces = []
    for at in range(0, v_ref.shape[1], 2 * LANES):
        cols = slice(at, at + 2 * LANES)
        grad = dot_nn(normed, jnp.where(first, vg0_ref[:, cols], vg1_ref[:, cols]))
        sloped = (grad * slope_ref[:, cols].astype(F32)).astype(BF16)
        pieces.append((v_ref[:, cols], sloped))
    both = dot_tn(*(jnp.concatenate(side, 0) for side in zip(*pieces)))
    total_ref[...] += both[:LANES, :LANES] + both[LANES:, LANES:]

    @pl.when(pl.program_id(0) == pl.num_programs(0) - 1)
    def _():
        total = (slope_factor * total_ref[...]).astype(out_ref.dtype)
        for i in range(out_ref.shape[0] // LANES):
            out_ref[i * LANES : (i + 1) * LANES] = total


def cayley_kernel(parts_ref, rot_ref, grad_ref, new_ref):
    count = parts_ref.shape[0] // LANES
    grad = parts_ref[:LANES].astype(F32)
    for i in range(1, count):
        grad = grad + parts_ref[i * LANES : (i + 1) * LANES].astype(F32)
    grad_ref[...] = grad
    rot = rot_ref[...]

    def product(a, b, dims=(1, 0)):
        return lax.dot_general(
            a, b, (((dims[0],), (dims[1],)), ((), ())), precision=precise, preferred_element_type=F32
        )

    turn = product(grad, rot, (1, 1))
    skew = turn - jnp.transpose(turn)
    update = rot - step_size * product(skew, rot)
    for _ in range(2):
        update = rot - 0.5 * step_size * product(skew, rot + update)
    new_ref[...] = update


def exchange(rows):
    return lax.all_to_all(rows, "tensor", split_axis=0, concat_axis=0, tiled=True)


def on_device(hidden, cotangent, norm_gain, value_weight, output_weight, rotation, attention):
    section = lax.axis_index("section")
    count = lax.axis_size("tensor")
    is_first = section == 0
    flag = section.astype(jnp.int32).reshape(1)
    rot = rotation[0]
    value_w = value_weight[0]
    out_w = output_weight[0]
    local, width = out_w.shape
    kv_width = value_w.shape[1]
    kv_count = kv_width // LANES
    tokens = hidden.shape[0]
    _, blocks, heads, flat = attention.shape
    seq = tokens // blocks
    probs = attention[0].reshape(blocks, heads * seq, seq)
    model_width = local * count
    big = 2 * tokens * local * width

    def split(rows, *tail):
        return pl.BlockSpec((rows,) + tail, lambda i: (i, 0))

    def across(lines, rows):
        return pl.BlockSpec((lines, rows), lambda i: (0, i))

    def whole(*shape):
        return pl.BlockSpec(shape, lambda i: (0,) * len(shape))

    rows = min(local, 256)
    half_rows = max(local // 2, min(local, 128))
    x0, ct, gain, value_rot, stat = call(
        value_rot_kernel,
        (
            shaped((local, tokens), BF16),
            shaped((local, tokens), BF16),
            shaped((local, tokens), F32),
            shaped((local, kv_width), F32),
            shaped((count, kv_width + tokens), F32),
        ),
        (4 * local * kv_width * LANES, 6 * local * kv_width),
        grid=(local // half_rows,),
        in_specs=[
            across(tokens, half_rows),
            across(tokens, half_rows),
            across(1, half_rows),
            split(half_rows, kv_width),
            whole(LANES, LANES),
        ],
        out_specs=(
            split(half_rows, tokens),
            split(half_rows, tokens),
            split(half_rows, tokens),
            split(half_rows, kv_width),
            whole(count, kv_width + tokens),
        ),
        scratch_shapes=[pltpu.VMEM((1, kv_width + tokens), F32)],
    )(hidden, cotangent, norm_gain, value_w, rot)
    stats = exchange(stat)

    part_rows = min(local, 256)
    part_count = local // part_rows

    def prepare(first, number, before):
        starts, ends = first == 0, first + number == part_count

        def ahead(lines, *tail):
            return pl.BlockSpec((lines,) + tail, lambda i: (first + i, 0))

        def behind(lines, *tail):
            return pl.BlockSpec((lines,) + tail, lambda i: (first + i, 0))

        anywhere = pl.BlockSpec(memory_space=pl.ANY)
        operands = [out_w, rot, ct]
        in_specs = [ahead(part_rows, width), whole(LANES, LANES), behind(part_rows, tokens)]
        if ends:
            operands.append(probs)
            in_specs.append(whole(*probs.shape))
        aliases = {}
        if not starts:
            quant, slope, held, after = before
            at = len(operands)
            operands += [after, held, quant, slope]
            in_specs += [anywhere, whole(tokens, width), anywhere, anywhere]
            aliases = {at + 2: 0, at + 3: 1}
        outs = [shaped((local, width), BF16), shaped((local, width), BF16)]
        out_specs = [behind(part_rows, width), behind(part_rows, width)]
        scratch = [pltpu.VMEM((tokens, width), F32)]
        if ends:
            outs += [shaped((tokens, width), BF16), shaped((tokens, kv_width), BF16)]
            out_specs += [whole(tokens, width), whole(tokens, kv_width)]
        else:
            outs.append(shaped((tokens, width), BF16))
            out_specs.append(whole(tokens, width))
        scratch += [
            pltpu.VMEM((part_rows, width), F32),
            pltpu.VMEM((part_rows, LANES), F32),
            pltpu.VMEM((part_rows, LANES), F32),
        ]
        return call(
            functools.partial(prep_kernel, kv_count, starts, ends, number),
            tuple(outs),
            (40 * big * number // part_count, 6 * local * width * number // part_count),
            grid=(number,),
            in_specs=in_specs,
            out_specs=tuple(out_specs),
            scratch_shapes=scratch,
            input_output_aliases=aliases,
        )(*operands)

    lead = part_count // 4
    before = prepare(0, lead, None) if lead else None

    value_q, value_slope, value_part, mean0 = call(
        functools.partial(value_quant_kernel, model_width),
        (
            shaped((local, kv_width), BF16),
            shaped((local, kv_width), BF16),
            shaped((tokens, kv_width), BF16),
            shaped((1, tokens), F32),
        ),
        (2 * local * kv_width * tokens, 8 * local * kv_width),
        grid=(local // half_rows,),
        in_specs=[
            split(half_rows, kv_width),
            whole(count, kv_width + tokens),
            split(half_rows, tokens),
            split(half_rows, tokens),
        ],
        out_specs=(
            split(half_rows, kv_width),
            split(half_rows, kv_width),
            whole(tokens, kv_width),
            whole(1, tokens),
        ),
        scratch_shapes=[pltpu.VMEM((tokens, kv_width), F32)],
    )(value_rot, stats, x0, gain)

    def add_parts(received):
        return received.reshape(count, tokens // count, -1).astype(F32).sum(0)

    def spread(part):
        return jnp.tile(part.astype(BF16), (count, 1))

    values0 = spread(add_parts(exchange(value_part)))
    if lead:
        before = tuple(before) + (value_part,)
    quant, slope, ct_back, ct_vg = prepare(lead, part_count - lead, before)

    on_first = 1 - flag
    anywhere = pl.BlockSpec(memory_space=pl.ANY)

    def only(lines, *tail):
        return pl.BlockSpec((lines,) + tail, lambda i, active: (i * active[0], 0))

    def each(lines, *tail):
        return pl.BlockSpec((lines,) + tail, lambda i, active: (i, 0))

    def fixed(*shape):
        return pl.BlockSpec(shape, lambda i, active: (0,) * len(shape))

    second = exchange(jnp.where(is_first, values0, ct_vg))
    second, to_gather = lax.optimization_barrier((second, spread(add_parts(second))))
    vg1 = exchange(to_gather)

    mixed, x1 = call(
        functools.partial(forward_kernel, kv_count),
        (shaped((tokens, width), BF16), shaped((local, tokens), BF16)),
        (big, 2 * local * width),
        prefetch=1,
        grid=(local // rows,),
        in_specs=[
            fixed(tokens, kv_width),
            fixed(*probs.shape),
            only(rows, width),
            only(rows, tokens),
        ],
        out_specs=(fixed(tokens, width), only(rows, tokens)),
    )(on_first, second, probs, quant, x0)
    arrived = lax.ppermute(x1, "section", [(0, 1)])

    projected, grad1 = call(
        project_kernel,
        (shaped((tokens, kv_width + tokens), BF16), shaped((local, tokens), BF16)),
        (4 * local * kv_width * tokens, 2 * local * kv_width),
        prefetch=1,
        grid=(local // half_rows,),
        in_specs=[
            each(half_rows, tokens),
            each(half_rows, tokens),
            fixed(tokens, kv_width),
            each(half_rows, tokens),
            only(half_rows, kv_width),
        ],
        out_specs=(fixed(tokens, kv_width + tokens), only(half_rows, tokens)),
        scratch_shapes=[pltpu.VMEM((tokens, kv_width), F32), pltpu.VMEM((1, tokens), F32)],
    )(flag, x1, arrived, vg1, gain, value_q)
    received = add_parts(exchange(projected))
    mean1 = lax.rsqrt(received[:1, kv_width:] / model_width + norm_eps)

    grad1 = lax.ppermute(grad1, "section", [(1, 0)])
    grad_back = call(
        back_kernel,
        shaped((tokens, width), BF16),
        (big, 2 * local * width),
        prefetch=1,
        grid=(local // rows,),
        in_specs=[only(rows, width), only(rows, tokens), anywhere],
        out_specs=fixed(tokens, width),
        scratch_shapes=[pltpu.VMEM((tokens, width), F32)],
    )(on_first, quant, grad1, projected)

    vg0 = call(
        functools.partial(value_grad_kernel, kv_count),
        shaped((tokens, kv_width), BF16),
        (2 * tokens * width * seq, 6 * tokens * width),
        prefetch=1,
        grid=(blocks,),
        in_specs=[
            fixed(1, tokens),
            each(seq, width),
            each(seq, width),
            pl.BlockSpec((1, heads * seq, seq), lambda i, active: (i, 0, 0)),
        ],
        out_specs=each(seq, kv_width),
        scratch_shapes=[pltpu.VMEM((tokens, tokens), F32)],
    )(on_first, mean1, ct_back, grad_back, probs)
    mine = lax.axis_index("tensor") * (tokens // count)
    own_mean = lax.dynamic_slice(mean1[0], (mine,), (tokens // count,))[:, None]
    to_send = jnp.where(is_first, vg0, spread(received[:, :kv_width] * own_mean))
    values1 = exchange(to_send)

    def early(lines, *tail):
        return pl.BlockSpec((lines,) + tail, lambda i, section: (i * (1 - section[0]), 0))

    half = local // rows // 2
    pair_total = pltpu.VMEM((2 * LANES, 2 * LANES), F32)
    out_part = jnp.zeros((LANES, LANES), F32)
    if half:
        out_part = call(
            early_grad_kernel,
            shaped((LANES, LANES), F32),
            (big, 2 * local * width),
            prefetch=1,
            grid=(half,),
            in_specs=[
                fixed(1, tokens),
                fixed(tokens, width),
                early(rows, tokens),
                early(rows, tokens),
                early(rows, width),
                early(rows, width),
                anywhere,
            ],
            out_specs=fixed(LANES, LANES),
            scratch_shapes=[pair_total],
        )(flag, mean1, mixed, ct, grad1, out_w, slope, to_send)
        values1, out_part = lax.optimization_barrier((values1, out_part))
    vg0 = exchange(spread(add_parts(values1)))

    def late(lines, *tail):
        return pl.BlockSpec(
            (lines,) + tail, lambda i, section: (jnp.maximum(i, (1 - section[0]) * half), 0)
        )

    out_part = call(
        functools.partial(out_grad_kernel, kv_count, half),
        shaped((LANES, LANES), F32),
        (2 * big, 4 * local * width),
        prefetch=1,
        grid=(local // rows,),
        in_specs=[
            fixed(tokens, kv_width),
            fixed(1, tokens),
            fixed(*probs.shape),
            fixed(tokens, width),
            late(rows, tokens),
            late(rows, tokens),
            late(rows, width),
            late(rows, width),
            fixed(LANES, LANES),
        ],
        out_specs=fixed(LANES, LANES),
        scratch_shapes=[pltpu.VMEM((tokens, width), BF16), pair_total],
    )(flag, values1, mean1, probs, mixed, ct, grad1, out_w, slope, out_part)

    rot_part = call(
        value_part_kernel,
        shaped((count * LANES, LANES), BF16),
        (4 * local * kv_width * tokens, 4 * local * kv_width),
        grid=(1,),
        in_specs=[
            pl.BlockSpec(memory_space=pltpu.SMEM),
            split(local, tokens),
            split(local, tokens),
            whole(1, tokens),
            whole(1, tokens),
            split(local, tokens),
            whole(tokens, kv_width),
            whole(tokens, kv_width),
            split(local, kv_width),
            split(local, kv_width),
            whole(LANES, LANES),
        ],
        out_specs=whole(count * LANES, LANES),
        scratch_shapes=[pltpu.VMEM((LANES, LANES), F32)],
    )(flag, x0, arrived, mean0, mean1, gain, vg0, vg1, value_w, value_slope, out_part)
    rot_grad, rot_new = call(
        cayley_kernel,
        (shaped((LANES, LANES), F32), shaped((LANES, LANES), F32)),
        (12 * 5 * LANES**3, 8 * LANES**2),
    )(exchange(rot_part), rot)
    return rot_grad[None], rot_new[None]


def solution(mesh):
    in_specs = (
        P("groups", "tensor"),
        P("groups", "tensor"),
        P("section", "tensor"),
        P("section", "tensor", None),
        P("section", "tensor", None),
        P("section", None, None),
        P("section", "groups", None, None),
    )
    out_specs = (P("section", "groups", None), P("section", "groups", None))
    return jax.shard_map(
        on_device, mesh=mesh, in_specs=in_specs, out_specs=out_specs, check_vma=False
    )
```

```python
import functools

import jax
import jax.numpy as jnp
from jax import lax
from jax.experimental import pallas as pl
from jax.experimental.pallas import tpu as pltpu
from jax.sharding import PartitionSpec as P

quant_levels = 7.0
norm_eps = 1e-05
scale_eps = 1e-06
step_size = 0.1
precise = lax.Precision.HIGHEST
F32 = jnp.float32
BF16 = jnp.bfloat16
LANES = 128
VMEM_BYTES = 56 * 1024 * 1024

sin_coefs = (3.141582078119497, -5.16714420271071, 2.541908924984016, -0.5546570710297597)
sin_top = sin_coefs[3]
slope_factor = 2.0 * sin_top * sin_top
unit = 1.000002 / (sin_top * sin_top)


def dot_nn(a, b):
    return lax.dot_general(a, b, (((1,), (0,)), ((), ())), preferred_element_type=F32)


def dot_nt(a, b):
    return lax.dot_general(a, b, (((1,), (1,)), ((), ())), preferred_element_type=F32)


def dot_tn(a, b):
    return lax.dot_general(a, b, (((0,), (0,)), ((), ())), preferred_element_type=F32)


def sine_scale(scale):
    return scale * (-sin_top * sin_top / 3.141592653589793)


def soft_parts(turned, inverse, factor):
    ratio = turned * inverse
    rest = ratio - jnp.round(ratio)
    square = rest * rest
    sine = rest * (
        ((square + sin_coefs[2] / sin_top) * square + sin_coefs[1] / sin_top) * square
        + sin_coefs[0] / sin_top
    )
    slope = sine * sine
    below = unit - slope
    return turned - (sine * (below * lax.rsqrt(below))) * factor, slope


def rotation_pair(rot):
    high = rot.astype(BF16)
    low = (rot - high.astype(F32)).astype(BF16)
    zero = jnp.zeros_like(high)

    def blocks(part):
        return jnp.concatenate(
            [jnp.concatenate([part, zero], 1), jnp.concatenate([zero, part], 1)], 0
        )

    return blocks(high), blocks(low)


def column_of(row):
    count = row.shape[1]
    return jnp.transpose(jnp.broadcast_to(row, (count, count)))


def call(kernel, out_shape, cost, **kw):
    flops, moved = cost
    prefetch = kw.pop("prefetch", 0)
    if prefetch:
        names = ("grid", "in_specs", "out_specs", "scratch_shapes")
        fields = {name: kw.pop(name) for name in names if name in kw}
        kw["grid_spec"] = pltpu.PrefetchScalarGridSpec(num_scalar_prefetch=prefetch, **fields)
    return pl.pallas_call(
        kernel,
        out_shape=out_shape,
        compiler_params=pltpu.CompilerParams(vmem_limit_bytes=VMEM_BYTES),
        cost_estimate=pl.CostEstimate(flops=flops, bytes_accessed=moved, transcendentals=0),
        **kw,
    )


def shaped(shape, dtype):
    return jax.ShapeDtypeStruct(shape, dtype)


def value_rot_kernel(
    hidden_ref, ct_ref, gain_row_ref, value_ref, rot_ref,
    x_ref, ct_t_ref, gain_ref, vrot_ref, stats_ref, stat_ref,
):
    kv_width = value_ref.shape[1]
    high, low = rotation_pair(rot_ref[...])

    @pl.when(pl.program_id(0) == 0)
    def _():
        stat_ref[...] = jnp.zeros_like(stat_ref)

    for at in range(0, kv_width, 2 * LANES):
        cols = slice(at, at + 2 * LANES)
        block = value_ref[:, cols]
        turned = dot_nn(block, high) + dot_nn(block, low)
        vrot_ref[:, cols] = turned
        peak = jnp.max(jnp.abs(turned), axis=0, keepdims=True)
        stat_ref[:, cols] = jnp.maximum(stat_ref[:, cols], peak)
    x = jnp.transpose(hidden_ref[...].astype(F32))
    x_ref[...] = x.astype(BF16)
    stat_ref[:, kv_width:] += jnp.sum(x * x, axis=0, keepdims=True)
    ct_t_ref[...] = jnp.transpose(ct_ref[...].astype(F32)).astype(BF16)
    gain_ref[...] = jnp.transpose(jnp.broadcast_to(gain_row_ref[...], hidden_ref.shape))

    @pl.when(pl.program_id(0) == pl.num_programs(0) - 1)
    def _():
        stats_ref[...] = jnp.broadcast_to(stat_ref[...], stats_ref.shape)


def mix_back(probs_ref, grad_of, out_ref, seq, per_group, kv_count):
    blocks = probs_ref.shape[0]
    for b in range(blocks):
        rows = slice(b * seq, (b + 1) * seq)
        for k in range(kv_count):
            stacked = jnp.concatenate(
                [
                    grad_of(rows, slice(h * LANES, (h + 1) * LANES))
                    for h in range(k * per_group, (k + 1) * per_group)
                ],
                0,
            )
            probs = probs_ref[b, k * per_group * seq : (k + 1) * per_group * seq, :]
            out_ref[rows, k * LANES : (k + 1) * LANES] = dot_tn(probs, stacked).astype(
                out_ref.dtype
            )


def mix_forward(probs_ref, values_of, mixed_ref, seq, per_group, kv_count):
    blocks = probs_ref.shape[0]
    for b in range(blocks):
        rows = slice(b * seq, (b + 1) * seq)
        for k in range(kv_count):
            probs = probs_ref[b, k * per_group * seq : (k + 1) * per_group * seq, :]
            heads = dot_nn(probs, values_of(rows, slice(k * LANES, (k + 1) * LANES))).astype(BF16)
            for j in range(per_group):
                h = k * per_group + j
                mixed_ref[rows, h * LANES : (h + 1) * LANES] = heads[j * seq : (j + 1) * seq]


def prep_kernel(kv_count, starts, ends, number, *refs):
    refs = list(refs)
    w_ref, rot_ref, ct_ref = refs[:3]
    del refs[:3]
    if ends:
        probs_ref = refs.pop(0)
    if not starts:
        held_ref = refs[1]
        del refs[:4]
    q_ref, slope_ref = refs[:2]
    del refs[:2]
    back_ref = refs.pop(0)
    if ends:
        vg_ref = refs.pop(0)
    total_ref, turned_ref, inv_ref, factor_ref = refs
    rows, width = w_ref.shape
    step, last = pl.program_id(0), number - 1
    lines = 16
    wide = min(1024, width)

    @pl.when(step == 0)
    def _():
        total_ref[...] = jnp.zeros_like(total_ref)

    high, low = rotation_pair(rot_ref[...])
    peak = jnp.zeros((rows, LANES), F32)
    for at in range(0, width, 2 * LANES):
        cols = slice(at, at + 2 * LANES)
        block = w_ref[:, cols]
        turned = dot_nn(block, high) + dot_nn(block, low)
        turned_ref[:, cols] = turned
        size = jnp.abs(turned)
        peak = jnp.maximum(peak, jnp.maximum(size[:, :LANES], size[:, LANES:]))
    scale = (jnp.max(peak, axis=1, keepdims=True) + scale_eps) / quant_levels
    inv_ref[...] = jnp.broadcast_to(1.0 / scale, inv_ref.shape)
    factor_ref[...] = jnp.broadcast_to(sine_scale(scale), inv_ref.shape)

    @pl.loop(0, rows // lines, unroll=4)
    def _(i):
        here = pl.ds(pl.multiple_of(i * lines, lines), lines)
        inverse, factor = inv_ref[here, :], factor_ref[here, :]
        for at in range(0, width, LANES):
            cols = slice(at, at + LANES)
            effective, slope = soft_parts(turned_ref[here, cols], inverse, factor)
            q_ref[here, cols] = effective.astype(BF16)
            slope_ref[here, cols] = slope.astype(BF16)

    for at in range(0, width, wide):
        cols = slice(at, at + wide)
        total_ref[:, cols] += dot_tn(ct_ref[...], q_ref[:, cols])

    if ends:

        @pl.when(step == last)
        def _():
            if not starts:
                total_ref[...] += held_ref[...].astype(F32)
            back_ref[...] = total_ref[...].astype(BF16)
            seq = probs_ref.shape[2]
            per_group = width // LANES // kv_count
            mix_back(probs_ref, lambda r, c: back_ref[r, c], vg_ref, seq, per_group, kv_count)
    else:

        @pl.when(step == last)
        def _():
            back_ref[...] = total_ref[...].astype(BF16)


def value_quant_kernel(
    model_width, turned_ref, stats_ref, x_ref, gain_ref, q_ref, slope_ref, part_ref, mean_ref, total_ref
):
    kv_width = turned_ref.shape[1]
    stats = stats_ref[...]
    scale = (jnp.max(stats[:, :kv_width], axis=0, keepdims=True) + scale_eps) / quant_levels
    squares = jnp.sum(stats[:, kv_width:], axis=0, keepdims=True)
    mean = lax.rsqrt(squares / model_width + norm_eps)
    inverse = 1.0 / scale
    factor = sine_scale(scale)
    lines = 16
    inverses = [
        jnp.broadcast_to(inverse[:, at : at + LANES], (lines, LANES))
        for at in range(0, kv_width, LANES)
    ]

    @pl.loop(0, turned_ref.shape[0] // lines)
    def _(i):
        here = pl.ds(pl.multiple_of(i * lines, lines), lines)
        for j, wide in enumerate(inverses):
            cols = slice(j * LANES, (j + 1) * LANES)
            effective, slope = soft_parts(turned_ref[here, cols], wide, factor[:, cols])
            q_ref[here, cols] = effective.astype(BF16)
            slope_ref[here, cols] = slope.astype(BF16)

    @pl.when(pl.program_id(0) == 0)
    def _():
        mean_ref[...] = mean
        total_ref[...] = jnp.zeros_like(total_ref)

    normed = (x_ref[...].astype(F32) * mean * gain_ref[...]).astype(BF16)
    total_ref[...] += dot_tn(normed, q_ref[...])

    @pl.when(pl.program_id(0) == pl.num_programs(0) - 1)
    def _():
        part_ref[...] = total_ref[...].astype(BF16)


def forward_kernel(kv_count, active_ref, values_ref, probs_ref, q_ref, x_ref, mixed_ref, out_ref):
    @pl.when(active_ref[0] == 1)
    def _():
        @pl.when(pl.program_id(0) == 0)
        def _():
            seq = probs_ref.shape[2]
            per_group = q_ref.shape[1] // LANES // kv_count
            mix_forward(
                probs_ref, lambda r, c: values_ref[r, c], mixed_ref, seq, per_group, kv_count
            )

        out_ref[...] = (x_ref[...].astype(F32) + dot_nt(q_ref[...], mixed_ref[...])).astype(BF16)


def back_kernel(active_ref, q_ref, grad_ref, after_ref, back_ref, total_ref):
    width = q_ref.shape[1]

    @pl.when(active_ref[0] == 1)
    def _():
        @pl.when(pl.program_id(0) == 0)
        def _():
            total_ref[...] = jnp.zeros_like(total_ref)

        wide = min(1024, width)
        for at in range(0, width, wide):
            cols = slice(at, at + wide)
            total_ref[:, cols] += dot_tn(grad_ref[...], q_ref[:, cols])

        @pl.when(pl.program_id(0) == pl.num_programs(0) - 1)
        def _():
            back_ref[...] = total_ref[...].astype(BF16)


def project_kernel(
    active_ref, own_ref, arrived_ref, vg_ref, gain_ref, q_ref, out_ref, grad_ref, total_ref, sum_ref
):
    kv_width = q_ref.shape[1]
    last_section = active_ref[0] == 1
    first, last = pl.program_id(0) == 0, pl.program_id(0) == pl.num_programs(0) - 1

    @pl.when(first)
    def _():
        total_ref[...] = jnp.zeros_like(total_ref)
        sum_ref[...] = jnp.zeros_like(sum_ref)

    x = jnp.where(last_section, arrived_ref[...], own_ref[...]).astype(F32)
    sum_ref[...] += jnp.sum(x * x, axis=0, keepdims=True)

    @pl.when(last_section)
    def _():
        total_ref[...] += dot_tn((x * gain_ref[...]).astype(BF16), q_ref[...])
        grad_ref[...] = (dot_nt(q_ref[...], vg_ref[...]) * gain_ref[...]).astype(BF16)

    @pl.when(last)
    def _():
        out_ref[:, :kv_width] = total_ref[...].astype(BF16)
        tokens = sum_ref.shape[1]
        out_ref[:, kv_width:] = jnp.broadcast_to(sum_ref[...], (tokens, tokens)).astype(BF16)


def value_grad_kernel(kv_count, active_ref, mean_ref, ct_back_ref, back_ref, probs_ref, out_ref, inv_ref):
    seq = probs_ref.shape[2]
    per_group = back_ref.shape[1] // LANES // kv_count

    @pl.when(active_ref[0] == 1)
    def _():
        inv_ref[...] = column_of(mean_ref[...])
        inverse = inv_ref[pl.ds(pl.multiple_of(pl.program_id(0) * seq, seq), seq), :1]

        def grad_of(rows, cols):
            return (
                ct_back_ref[rows, cols].astype(F32) + inverse * back_ref[rows, cols].astype(F32)
            ).astype(BF16)

        mix_back(probs_ref, grad_of, out_ref, seq, per_group, kv_count)


def out_grad_block(grad, mixed_ref, w_ref, slope_ref, total_ref):
    width, together = w_ref.shape[1], 4
    for first in range(0, width, 2 * LANES * together):
        pieces = []
        for at in range(first, min(first + 2 * LANES * together, width), 2 * LANES):
            cols = slice(at, at + 2 * LANES)
            out_grad = dot_nn(grad, mixed_ref[:, cols])
            sloped = (out_grad * slope_ref[:, cols].astype(F32)).astype(BF16)
            pieces.append((w_ref[:, cols], sloped))
        total_ref[...] += dot_tn(*(jnp.concatenate(side, 0) for side in zip(*pieces)))


def both_heads(total_ref):
    return total_ref[:LANES, :LANES] + total_ref[LANES:, LANES:]


def early_grad_kernel(
    section_ref, mean_ref, mixed_ref, ct_ref, grad_ref, w_ref, slope_ref, after_ref, out_ref, total_ref
):
    @pl.when(pl.program_id(0) == 0)
    def _():
        total_ref[...] = jnp.zeros_like(total_ref)

    @pl.when(section_ref[0] == 0)
    def _():
        grad = (ct_ref[...].astype(F32) + mean_ref[...] * grad_ref[...].astype(F32)).astype(BF16)
        out_grad_block(grad, mixed_ref, w_ref, slope_ref, total_ref)

    @pl.when(pl.program_id(0) == pl.num_programs(0) - 1)
    def _():
        out_ref[...] = both_heads(total_ref)


def out_grad_kernel(
    kv_count, half, section_ref, values_ref, mean_ref, probs_ref, mixed_in_ref,
    ct_ref, grad_ref, w_ref, slope_ref, other_ref, out_ref, mixed_ref, total_ref,
):
    seq = probs_ref.shape[2]
    per_group = w_ref.shape[1] // LANES // kv_count
    last_section = section_ref[0] != 0

    @pl.when(pl.program_id(0) == 0)
    def _():
        total_ref[...] = jnp.zeros_like(total_ref)

        @pl.when(last_section)
        def _():
            mix_forward(
                probs_ref, lambda r, c: values_ref[r, c], mixed_ref, seq, per_group, kv_count
            )

    @pl.when(last_section)
    def _():
        out_grad_block(ct_ref[...], mixed_ref, w_ref, slope_ref, total_ref)

    @pl.when(jnp.logical_and(section_ref[0] == 0, pl.program_id(0) >= half))
    def _():
        grad = (ct_ref[...].astype(F32) + mean_ref[...] * grad_ref[...].astype(F32)).astype(BF16)
        out_grad_block(grad, mixed_in_ref, w_ref, slope_ref, total_ref)

    @pl.when(pl.program_id(0) == pl.num_programs(0) - 1)
    def _():
        out_ref[...] = both_heads(total_ref)
        if half:
            out_ref[...] += other_ref[...]


def value_part_kernel(
    section_ref, x0_ref, x1_ref, mean0_ref, mean1_ref, gain_ref, vg0_ref, vg1_ref, v_ref, slope_ref,
    other_ref, out_ref, total_ref,
):
    first = section_ref[0] == 0
    x = jnp.where(first, x0_ref[...], x1_ref[...]).astype(F32)
    mean = jnp.where(first, mean0_ref[...], mean1_ref[...])
    normed = (x * mean * gain_ref[...]).astype(BF16)

    @pl.when(pl.program_id(0) == 0)
    def _():
        total_ref[...] = other_ref[...]

    pieces = []
    for at in range(0, v_ref.shape[1], 2 * LANES):
        cols = slice(at, at + 2 * LANES)
        grad = dot_nn(normed, jnp.where(first, vg0_ref[:, cols], vg1_ref[:, cols]))
        sloped = (grad * slope_ref[:, cols].astype(F32)).astype(BF16)
        pieces.append((v_ref[:, cols], sloped))
    both = dot_tn(*(jnp.concatenate(side, 0) for side in zip(*pieces)))
    total_ref[...] += both[:LANES, :LANES] + both[LANES:, LANES:]

    @pl.when(pl.program_id(0) == pl.num_programs(0) - 1)
    def _():
        total = (slope_factor * total_ref[...]).astype(out_ref.dtype)
        for i in range(out_ref.shape[0] // LANES):
            out_ref[i * LANES : (i + 1) * LANES] = total


def cayley_kernel(parts_ref, rot_ref, grad_ref, new_ref):
    count = parts_ref.shape[0] // LANES
    grad = parts_ref[:LANES].astype(F32)
    for i in range(1, count):
        grad = grad + parts_ref[i * LANES : (i + 1) * LANES].astype(F32)
    grad_ref[...] = grad
    rot = rot_ref[...]

    def product(a, b, dims=(1, 0)):
        return lax.dot_general(
            a, b, (((dims[0],), (dims[1],)), ((), ())), precision=precise, preferred_element_type=F32
        )

    turn = product(grad, rot, (1, 1))
    skew = turn - jnp.transpose(turn)
    update = rot - step_size * product(skew, rot)
    for _ in range(2):
        update = rot - 0.5 * step_size * product(skew, rot + update)
    new_ref[...] = update


def exchange(rows):
    return lax.all_to_all(rows, "tensor", split_axis=0, concat_axis=0, tiled=True)


def on_device(hidden, cotangent, norm_gain, value_weight, output_weight, rotation, attention):
    section = lax.axis_index("section")
    count = lax.axis_size("tensor")
    is_first = section == 0
    flag = section.astype(jnp.int32).reshape(1)
    rot = rotation[0]
    value_w = value_weight[0]
    out_w = output_weight[0]
    local, width = out_w.shape
    kv_width = value_w.shape[1]
    kv_count = kv_width // LANES
    tokens = hidden.shape[0]
    _, blocks, heads, flat = attention.shape
    seq = tokens // blocks
    probs = attention[0].reshape(blocks, heads * seq, seq)
    model_width = local * count
    big = 2 * tokens * local * width

    def split(rows, *tail):
        return pl.BlockSpec((rows,) + tail, lambda i: (i, 0))

    def across(lines, rows):
        return pl.BlockSpec((lines, rows), lambda i: (0, i))

    def whole(*shape):
        return pl.BlockSpec(shape, lambda i: (0,) * len(shape))

    rows = min(local, 256)
    half_rows = max(local // 2, min(local, 128))
    x0, ct, gain, value_rot, stat = call(
        value_rot_kernel,
        (
            shaped((local, tokens), BF16),
            shaped((local, tokens), BF16),
            shaped((local, tokens), F32),
            shaped((local, kv_width), F32),
            shaped((count, kv_width + tokens), F32),
        ),
        (4 * local * kv_width * LANES, 6 * local * kv_width),
        grid=(local // half_rows,),
        in_specs=[
            across(tokens, half_rows),
            across(tokens, half_rows),
            across(1, half_rows),
            split(half_rows, kv_width),
            whole(LANES, LANES),
        ],
        out_specs=(
            split(half_rows, tokens),
            split(half_rows, tokens),
            split(half_rows, tokens),
            split(half_rows, kv_width),
            whole(count, kv_width + tokens),
        ),
        scratch_shapes=[pltpu.VMEM((1, kv_width + tokens), F32)],
    )(hidden, cotangent, norm_gain, value_w, rot)
    stats = exchange(stat)

    part_rows = min(local, 256)
    part_count = local // part_rows

    def prepare(first, number, before):
        starts, ends = first == 0, first + number == part_count

        def ahead(lines, *tail):
            return pl.BlockSpec((lines,) + tail, lambda i: (first + i, 0))

        def behind(lines, *tail):
            return pl.BlockSpec((lines,) + tail, lambda i: (first + i, 0))

        anywhere = pl.BlockSpec(memory_space=pl.ANY)
        operands = [out_w, rot, ct]
        in_specs = [ahead(part_rows, width), whole(LANES, LANES), behind(part_rows, tokens)]
        if ends:
            operands.append(probs)
            in_specs.append(whole(*probs.shape))
        aliases = {}
        if not starts:
            quant, slope, held, after = before
            at = len(operands)
            operands += [after, held, quant, slope]
            in_specs += [anywhere, whole(tokens, width), anywhere, anywhere]
            aliases = {at + 2: 0, at + 3: 1}
        outs = [shaped((local, width), BF16), shaped((local, width), BF16)]
        out_specs = [behind(part_rows, width), behind(part_rows, width)]
        scratch = [pltpu.VMEM((tokens, width), F32)]
        if ends:
            outs += [shaped((tokens, width), BF16), shaped((tokens, kv_width), BF16)]
            out_specs += [whole(tokens, width), whole(tokens, kv_width)]
        else:
            outs.append(shaped((tokens, width), BF16))
            out_specs.append(whole(tokens, width))
        scratch += [
            pltpu.VMEM((part_rows, width), F32),
            pltpu.VMEM((part_rows, LANES), F32),
            pltpu.VMEM((part_rows, LANES), F32),
        ]
        return call(
            functools.partial(prep_kernel, kv_count, starts, ends, number),
            tuple(outs),
            (40 * big * number // part_count, 6 * local * width * number // part_count),
            grid=(number,),
            in_specs=in_specs,
            out_specs=tuple(out_specs),
            scratch_shapes=scratch,
            input_output_aliases=aliases,
        )(*operands)

    lead = part_count // 4
    before = prepare(0, lead, None) if lead else None

    value_q, value_slope, value_part, mean0 = call(
        functools.partial(value_quant_kernel, model_width),
        (
            shaped((local, kv_width), BF16),
            shaped((local, kv_width), BF16),
            shaped((tokens, kv_width), BF16),
            shaped((1, tokens), F32),
        ),
        (2 * local * kv_width * tokens, 8 * local * kv_width),
        grid=(local // half_rows,),
        in_specs=[
            split(half_rows, kv_width),
            whole(count, kv_width + tokens),
            split(half_rows, tokens),
            split(half_rows, tokens),
        ],
        out_specs=(
            split(half_rows, kv_width),
            split(half_rows, kv_width),
            whole(tokens, kv_width),
            whole(1, tokens),
        ),
        scratch_shapes=[pltpu.VMEM((tokens, kv_width), F32)],
    )(value_rot, stats, x0, gain)

    def add_parts(received):
        return received.reshape(count, tokens // count, -1).astype(F32).sum(0)

    def spread(part):
        return jnp.tile(part.astype(BF16), (count, 1))

    values0 = spread(add_parts(exchange(value_part)))
    if lead:
        before = tuple(before) + (value_part,)
    quant, slope, ct_back, ct_vg = prepare(lead, part_count - lead, before)

    on_first = 1 - flag
    anywhere = pl.BlockSpec(memory_space=pl.ANY)

    def only(lines, *tail):
        return pl.BlockSpec((lines,) + tail, lambda i, active: (i * active[0], 0))

    def each(lines, *tail):
        return pl.BlockSpec((lines,) + tail, lambda i, active: (i, 0))

    def fixed(*shape):
        return pl.BlockSpec(shape, lambda i, active: (0,) * len(shape))

    second = exchange(jnp.where(is_first, values0, ct_vg))
    second, to_gather = lax.optimization_barrier((second, spread(add_parts(second))))
    vg1 = exchange(to_gather)

    mixed, x1 = call(
        functools.partial(forward_kernel, kv_count),
        (shaped((tokens, width), BF16), shaped((local, tokens), BF16)),
        (big, 2 * local * width),
        prefetch=1,
        grid=(local // rows,),
        in_specs=[
            fixed(tokens, kv_width),
            fixed(*probs.shape),
            only(rows, width),
            only(rows, tokens),
        ],
        out_specs=(fixed(tokens, width), only(rows, tokens)),
    )(on_first, second, probs, quant, x0)
    arrived = lax.ppermute(x1, "section", [(0, 1)])

    projected, grad1 = call(
        project_kernel,
        (shaped((tokens, kv_width + tokens), BF16), shaped((local, tokens), BF16)),
        (4 * local * kv_width * tokens, 2 * local * kv_width),
        prefetch=1,
        grid=(local // half_rows,),
        in_specs=[
            each(half_rows, tokens),
            each(half_rows, tokens),
            fixed(tokens, kv_width),
            each(half_rows, tokens),
            only(half_rows, kv_width),
        ],
        out_specs=(fixed(tokens, kv_width + tokens), only(half_rows, tokens)),
        scratch_shapes=[pltpu.VMEM((tokens, kv_width), F32), pltpu.VMEM((1, tokens), F32)],
    )(flag, x1, arrived, vg1, gain, value_q)
    received = add_parts(exchange(projected))
    mean1 = lax.rsqrt(received[:1, kv_width:] / model_width + norm_eps)

    grad1 = lax.ppermute(grad1, "section", [(1, 0)])
    grad_back = call(
        back_kernel,
        shaped((tokens, width), BF16),
        (big, 2 * local * width),
        prefetch=1,
        grid=(local // rows,),
        in_specs=[only(rows, width), only(rows, tokens), anywhere],
        out_specs=fixed(tokens, width),
        scratch_shapes=[pltpu.VMEM((tokens, width), F32)],
    )(on_first, quant, grad1, projected)

    vg0 = call(
        functools.partial(value_grad_kernel, kv_count),
        shaped((tokens, kv_width), BF16),
        (2 * tokens * width * seq, 6 * tokens * width),
        prefetch=1,
        grid=(blocks,),
        in_specs=[
            fixed(1, tokens),
            each(seq, width),
            each(seq, width),
            pl.BlockSpec((1, heads * seq, seq), lambda i, active: (i, 0, 0)),
        ],
        out_specs=each(seq, kv_width),
        scratch_shapes=[pltpu.VMEM((tokens, tokens), F32)],
    )(on_first, mean1, ct_back, grad_back, probs)
    mine = lax.axis_index("tensor") * (tokens // count)
    own_mean = lax.dynamic_slice(mean1[0], (mine,), (tokens // count,))[:, None]
    to_send = jnp.where(is_first, vg0, spread(received[:, :kv_width] * own_mean))
    values1 = exchange(to_send)

    def early(lines, *tail):
        return pl.BlockSpec((lines,) + tail, lambda i, section: (i * (1 - section[0]), 0))

    half = local // rows // 2
    pair_total = pltpu.VMEM((2 * LANES, 2 * LANES), F32)
    out_part = jnp.zeros((LANES, LANES), F32)
    if half:
        out_part = call(
            early_grad_kernel,
            shaped((LANES, LANES), F32),
            (big, 2 * local * width),
            prefetch=1,
            grid=(half,),
            in_specs=[
                fixed(1, tokens),
                fixed(tokens, width),
                early(rows, tokens),
                early(rows, tokens),
                early(rows, width),
                early(rows, width),
                anywhere,
            ],
            out_specs=fixed(LANES, LANES),
            scratch_shapes=[pair_total],
        )(flag, mean1, mixed, ct, grad1, out_w, slope, to_send)
        values1, out_part = lax.optimization_barrier((values1, out_part))
    vg0 = exchange(spread(add_parts(values1)))

    def late(lines, *tail):
        return pl.BlockSpec(
            (lines,) + tail, lambda i, section: (jnp.maximum(i, (1 - section[0]) * half), 0)
        )

    out_part = call(
        functools.partial(out_grad_kernel, kv_count, half),
        shaped((LANES, LANES), F32),
        (2 * big, 4 * local * width),
        prefetch=1,
        grid=(local // rows,),
        in_specs=[
            fixed(tokens, kv_width),
            fixed(1, tokens),
            fixed(*probs.shape),
            fixed(tokens, width),
            late(rows, tokens),
            late(rows, tokens),
            late(rows, width),
            late(rows, width),
            fixed(LANES, LANES),
        ],
        out_specs=fixed(LANES, LANES),
        scratch_shapes=[pltpu.VMEM((tokens, width), BF16), pair_total],
    )(flag, values1, mean1, probs, mixed, ct, grad1, out_w, slope, out_part)

    rot_part = call(
        value_part_kernel,
        shaped((count * LANES, LANES), BF16),
        (4 * local * kv_width * tokens, 4 * local * kv_width),
        grid=(1,),
        in_specs=[
            pl.BlockSpec(memory_space=pltpu.SMEM),
            split(local, tokens),
            split(local, tokens),
            whole(1, tokens),
            whole(1, tokens),
            split(local, tokens),
            whole(tokens, kv_width),
            whole(tokens, kv_width),
            split(local, kv_width),
            split(local, kv_width),
            whole(LANES, LANES),
        ],
        out_specs=whole(count * LANES, LANES),
        scratch_shapes=[pltpu.VMEM((LANES, LANES), F32)],
    )(flag, x0, arrived, mean0, mean1, gain, vg0, vg1, value_w, value_slope, out_part)
    rot_grad, rot_new = call(
        cayley_kernel,
        (shaped((LANES, LANES), F32), shaped((LANES, LANES), F32)),
        (12 * 5 * LANES**3, 8 * LANES**2),
    )(exchange(rot_part), rot)
    return rot_grad[None], rot_new[None]


def solution(mesh):
    in_specs = (
        P("groups", "tensor"),
        P("groups", "tensor"),
        P("section", "tensor"),
        P("section", "tensor", None),
        P("section", "tensor", None),
        P("section", None, None),
        P("section", "groups", None, None),
    )
    out_specs = (P("section", "groups", None), P("section", "groups", None))
    return jax.shard_map(
        on_device, mesh=mesh, in_specs=in_specs, out_specs=out_specs, check_vma=False
    )
```
